1024 devices in a mesh: replica: 64 (over z, core), tensor: 16 (over x, y).
Axes of the slice: x: 4, y: 4, z: 32, core: 2. Of those that a mesh axis runs over, the one named last changes fastest.
Arguments:
- activations: bfloat16 [16384, 4096], P('replica'), may hold values from -6 to 6
- out_grads: bfloat16 [16384, 4096], P('replica', 'tensor'), may hold values from -1 to 1
- query_weight: bfloat16 [4096, 4096], P(None, 'tensor'), may hold values from -0.375 to 0.375
- carried_q: float32 [4096, 64], P('tensor'), may hold values from -6 to 6
Outputs:
- input_grads: bfloat16 [16384, 4096], P(('replica', 'tensor'))
- q_summed: float32 [4096, 64], P('tensor')
- new_error: bfloat16 [64, 4096, 4096], P('replica', None, 'tensor')
The draws below stay inside these ranges and needn't reach their ends.
All inputs are finite; a program needn't handle non-finite values.
Results may differ from the reference program's by a relative error of at most 0.014.
Values may be sent and summed in bfloat16 or wider, within the bound.
A program may use at most 64 MiB of HBM per device.

```python
import jax
import jax.numpy as jnp
from jax import lax

D_WIN = 4096
COLS_DEV = 256
RANK = 64
TOK = 256
TOKENS = 16384
COLS_ALL = 4096
N_REPLICA = 64
N_TENSOR = 16


def spiked(array, own_key, source, target, blocks, factor):
    def block_of(position):
        return (jnp.arange(array.shape[position]) // (array.shape[position] // blocks)).reshape((-1,) + (1,) * (array.ndim - 1 - position))

    near = jax.random.permutation(own_key, blocks)[block_of(target)]
    other_side = (block_of(target) + blocks // 2) % blocks
    return jnp.where((block_of(source) == near) | (block_of(source) == other_side), factor * array, array)


def block_scale(key, dims, shards, low, high):
    def one(position, blocks):
        draws = jax.random.uniform(jax.random.fold_in(jax.random.fold_in(key, 6), position), (blocks,), jnp.float32, low / len(shards), high / len(shards))
        return jnp.repeat(jnp.exp(draws), dims[position] // blocks).reshape((-1,) + (1,) * (len(dims) - position - 1))

    gain = one(*shards[0])
    for cut in shards[1:]:
        gain = gain * one(*cut)
    return gain


def normal_values(key, dims, scale, bound, cuts=(), kind=jnp.bfloat16):
    level = block_scale(key, dims, cuts, -0.22, 0.18) if cuts else 1.0
    drawn = jax.random.normal(key, dims, jnp.float32) * scale * level
    return jnp.minimum(jnp.maximum(drawn, -bound), bound).astype(kind)


def heavy_noise(own_key, extent, spread, reach, cuts, heavy, held_as=jnp.bfloat16):
    entries = spread * jax.random.normal(own_key, extent, jnp.float32)
    if cuts:
        entries = entries * block_scale(own_key, extent, cuts, -0.22, 0.18)
    return jnp.clip(spiked(entries, jax.random.fold_in(own_key, 3), *heavy), -reach, reach).astype(held_as)


def setup_inputs(seed: int = 0) -> dict:
    seeds = jax.random.split(jax.random.key(seed), 5)
    return {
        "activations": normal_values(seeds[0], (TOKENS, D_WIN), 1.0, 6.0, ((0, 64),)),
        "out_grads": heavy_noise(seeds[1], (TOKENS, COLS_ALL), 0.125, 1.0, ((0, 64), (1, 16)), (1, 0, 64, 4.0)),
        "query_weight": normal_values(seeds[2], (D_WIN, COLS_ALL), COLS_DEV ** -0.5, 0.375, ((1, 16),)),
        "carried_q": normal_values(seeds[3], (COLS_ALL, RANK), 1.0, 6.0, ((0, 16),), jnp.float32),
    }


def orthonormalize(p_whole):
    gram_matrix = jnp.dot(p_whole.T.astype(jnp.float32), p_whole.astype(jnp.float32), precision=lax.Precision.HIGHEST, preferred_element_type=jnp.float32)
    cholesky_factor = jnp.linalg.cholesky(gram_matrix)
    return jax.scipy.linalg.solve_triangular(cholesky_factor, p_whole.T, lower=True).T

def reference(activations, out_grads, query_weight, carried_q):
    highest = lax.Precision.HIGHEST
    replica_inputs = activations.reshape(N_REPLICA, TOK, D_WIN).astype(jnp.float32)
    grouped_grads = jnp.transpose(out_grads.reshape(TOKENS, N_TENSOR, COLS_DEV), (1, 0, 2))
    grouped_weights = jnp.transpose(query_weight.reshape(D_WIN, N_TENSOR, COLS_DEV), (1, 0, 2))
    grouped_q = carried_q.reshape(N_TENSOR, COLS_DEV, RANK)

    def one_group(summed, pieces):
        grad_group, weight_group, q_group = pieces
        replica_grads = grad_group.reshape(N_REPLICA, TOK, COLS_DEV).astype(jnp.float32)
        gradient = jnp.einsum('rtd,rtc->rdc', replica_inputs, replica_grads, precision=highest)
        p_whole = jnp.einsum('rdc,ck->dk', gradient, q_group, precision=highest)
        p_orth = orthonormalize(p_whole)
        q_group_sum = jnp.einsum('rdc,dk->ck', gradient, p_orth, precision=highest)
        decompressed = jnp.dot(p_orth.astype(jnp.float32), q_group_sum.T.astype(jnp.float32), precision=highest, preferred_element_type=jnp.float32)
        error_group = (gradient - decompressed[None] / N_REPLICA).astype(jnp.bfloat16)
        partial_term = lax.dot_general(grad_group.astype(jnp.float32), weight_group.astype(jnp.float32), (((1,), (1,)), ((), ())), preferred_element_type=jnp.float32)
        summed = summed + partial_term.astype(jnp.bfloat16).astype(jnp.float32)
        return (summed, (q_group_sum, error_group))
    start_sum = jnp.zeros((TOKENS, D_WIN), jnp.float32)
    summed, (q_groups, error_groups) = lax.scan(one_group, start_sum, (grouped_grads, grouped_weights, grouped_q))
    input_grads = summed.astype(jnp.bfloat16)
    q_summed = q_groups.reshape(COLS_ALL, RANK)
    new_error = jnp.transpose(error_groups, (1, 2, 0, 3)).reshape(N_REPLICA, D_WIN, COLS_ALL)
    return (input_grads, q_summed, new_error)
```

```python
import functools

import jax
import jax.numpy as jnp
from jax import lax
from jax.experimental import pallas as pl
from jax.experimental.pallas import tpu as pltpu
from jax.sharding import PartitionSpec as P

MESH = pl.DeviceIdType.MESH
F32 = jnp.float32
BF16 = jnp.bfloat16

D_WIN = 4096
COLS = 256
TOK = 256
RANK = 64
CHIPS = 32
WIN = 8
GROUPS = CHIPS // WIN
PEERS = 16
BLK = D_WIN // (2 * WIN)
ROWS = TOK // PEERS

NEAR = (-4, 3, -3, 2, -2, 1, -1)
FAR = (16, 8, 24)


def dot(a, b, dims, precision=None):
    return lax.dot_general(a, b, (dims, ((), ())), precision=precision, preferred_element_type=F32)


def halves(x):
    high = x.astype(BF16)
    return high, (x - high.astype(F32)).astype(BF16)


def kernel(
    act_hbm, grad_hbm, weight_hbm, q_hbm,
    summed_hbm, q_out_hbm, error_hbm,
    act, og, weight, carried, gradient, part, from_peers, summed,
    p_send, p_acc, p_pair, near_send, near_recv, mid, p_full, p_cols, aug,
    s_send, s_pair, s_acc, s_near_recv, s_mid, s_full, q_out, error,
    load_sems, act_sems, store_sems, peer_send, peer_recv,
    pair_sems, near_s, near_r, mid_s, mid_r, gather_s, gather_r, pass_s, pass_r,
    s_pair_sems, s_near_s, s_near_r, s_mid_s, s_mid_r, s_gather_s, s_gather_r, s_pass_s, s_pass_r,
):
    replica = lax.axis_index("replica")
    tensor = lax.axis_index("tensor")
    chip = replica // 2
    core = lax.rem(replica, 2)
    other = 1 - core
    mine = lax.rem(chip, WIN)
    group = chip // WIN

    def at(offset):
        return (lax.rem(chip + offset + CHIPS, CHIPS) * 2 + core, tensor)

    partner = (chip * 2 + other, tensor)

    def peer(offset):
        return (replica, lax.rem(tensor + offset, PEERS))

    def remote(src, dst, send, recv, device):
        return pltpu.make_async_remote_copy(
            src_ref=src, dst_ref=dst, send_sem=send, recv_sem=recv, device_id=device, device_id_type=MESH
        )

    barrier = pltpu.get_barrier_semaphore()
    friends = [at(o) for o in FAR + (-4, 4, -3, 3, -2, 2, -1, 1)]
    friends += [peer(o) for o in range(1, PEERS)] + [partner]
    for friend in friends:
        pl.semaphore_signal(barrier, inc=1, device_id=friend, device_id_type=MESH)

    load_og = pltpu.make_async_copy(grad_hbm, og, load_sems.at[0])
    load_q = pltpu.make_async_copy(q_hbm, carried, load_sems.at[1])
    load_weight = pltpu.make_async_copy(weight_hbm, weight, load_sems.at[2])
    load_og.start()
    load_q.start()

    def load_act(index):
        half, j = index // WIN, lax.rem(index, WIN)
        b = 2 * j + lax.rem(half + other, 2)
        return pltpu.make_async_copy(act_hbm.at[:, pl.ds(b * BLK, BLK)], act.at[b], act_sems.at[index])

    @pl.loop(0, 2 * WIN)
    def _(i):
        load_act(i).start()

    load_weight.start()

    load_og.wait()
    load_q.wait()
    q_high, q_low = halves(carried[...])
    y2 = dot(jnp.concatenate([q_high, q_low], axis=0), og[...], ((1,), (1,)))
    y_high, y_low = halves(y2[:RANK] + y2[RANK:])
    y_parts = jnp.concatenate([y_high, y_low], axis=0)

    def p_block(i, b):
        load_act(i).wait()
        both = dot(y_parts, act[b], ((1,), (0,)))
        return both[:RANK] + both[RANK:]

    @pl.loop(0, WIN)
    def _(j):
        p_send[j] = p_block(j, 2 * j + other).astype(BF16)

    @pl.loop(0, WIN)
    def _(j):
        p_acc[j] = p_block(WIN + j, 2 * j + core)

    pl.semaphore_wait(barrier, len(friends))

    pair = remote(p_send, p_pair, pair_sems.at[0], pair_sems.at[1], partner)
    pair.start()

    load_weight.wait()

    @pl.loop(0, D_WIN // COLS)
    def _(b):
        rows = pl.ds(pl.multiple_of(b * COLS, COLS), COLS)
        part[:, rows] = dot(og[...], weight[rows, :], ((1,), (1,))).astype(BF16)

    pair.wait_recv()
    sends = []
    for k, e in enumerate(NEAR):
        j = lax.rem(chip + e + CHIPS, WIN)
        near_send[k] = (p_acc[j] + p_pair[j].astype(F32)).astype(BF16)
        copy = remote(near_send.at[k], near_recv.at[k], near_s.at[k], near_r.at[k], at(e))
        copy.start()
        sends.append(copy)

    peer_copies = []
    for o in range(1, PEERS):
        to = lax.rem(tensor + o, PEERS)
        copy = remote(
            part.at[pl.ds(pl.multiple_of(to * ROWS, ROWS), ROWS)], from_peers.at[tensor],
            peer_send.at[o - 1], peer_recv.at[o - 1], peer(o),
        )
        copy.start()
        peer_copies.append(copy)

    total = p_acc[mine] + p_pair[mine].astype(F32)
    for k in reversed(range(len(NEAR))):
        sends[k].wait_recv()
        total += near_recv[k].astype(F32)

    mid[group] = total.astype(BF16)
    mid_copies = []
    for k, o in enumerate(FAR):
        copy = remote(mid.at[group], mid.at[group], mid_s.at[k], mid_r.at[k], at(o))
        copy.start()
        mid_copies.append(copy)

    @pl.loop(0, D_WIN // BLK)
    def _(b):
        gradient[b] = dot(act[b], og[...], ((0,), (0,)))

    for copy in mid_copies:
        copy.wait_recv()
    chunk = mid[0].astype(F32)
    for g in range(1, GROUPS):
        chunk += mid[g].astype(F32)
    p_full[core, mine] = chunk.astype(BF16)

    def gather_from(k):
        return lax.rem(chip + NEAR[k] + CHIPS, WIN)

    gathers, passes = [], []
    for k, e in enumerate(NEAR):
        copy = remote(
            p_full.at[core, mine], p_full.at[core, mine], gather_s.at[k], gather_r.at[k], at(-e)
        )
        copy.start()
        gathers.append(copy)

    def hand_on(k, j):
        copy = remote(p_full.at[core, j], p_full.at[core, j], pass_s.at[k], pass_r.at[k], partner)
        copy.start()
        passes.append(copy)

    hand_on(len(NEAR), mine)

    def z_gram(half, j, carry):
        z, gram = carry
        block = p_full[half, j]
        return (
            z + dot(block, act[2 * j + half], ((1,), (1,))),
            gram + dot(block, block, ((1,), (1,))),
        )

    carry = (jnp.zeros((RANK, TOK), F32), jnp.zeros((RANK, RANK), F32))
    order = list(reversed(range(len(NEAR))))
    for k in order:
        remote(
            p_full.at[core, gather_from(k)], p_full.at[core, gather_from(k)],
            gather_s.at[k], gather_r.at[k], at(NEAR[k]),
        ).wait_recv()
        hand_on(k, gather_from(k))
    for k in [len(NEAR)] + order:
        j = mine if k == len(NEAR) else gather_from(k)
        remote(
            p_full.at[other, j], p_full.at[other, j], pass_s.at[k], pass_r.at[k], partner
        ).wait_recv()

    def z_step(i, carry):
        return z_gram(i // WIN, lax.rem(i, WIN), carry)

    z, gram = lax.fori_loop(0, 2 * WIN, z_step, carry)

    z_high, z_low = halves(z)
    s2 = dot(jnp.concatenate([z_high, z_low], axis=0), og[...], ((1,), (0,)))
    s = s2[:RANK] + s2[RANK:]
    half_cols = COLS // 2
    s_send[0] = s[:, :half_cols]
    s_send[1] = s[:, half_cols:]
    s_pair_copy = remote(s_send.at[other], s_pair, s_pair_sems.at[0], s_pair_sems.at[1], partner)
    s_pair_copy.start()
    lane = lax.broadcasted_iota(jnp.int32, (RANK, 2 * RANK), 1)
    row = lax.broadcasted_iota(jnp.int32, (RANK, 2 * RANK), 0)
    aug[:, :] = jnp.concatenate([gram, (lane == row)[:, :RANK].astype(F32)], axis=1)
    s_pair_copy.wait_recv()
    s_acc[...] = s_send[core] + s_pair[...]

    s_sends = []
    for k, e in enumerate(NEAR):
        j = lax.rem(chip + e + CHIPS, WIN)
        copy = remote(
            s_acc.at[pl.ds(pl.multiple_of(j * 8, 8), 8)], s_near_recv.at[k], s_near_s.at[k], s_near_r.at[k], at(e)
        )
        copy.start()
        s_sends.append(copy)

    s_total = s_acc[pl.ds(pl.multiple_of(mine * 8, 8), 8)]
    for k in order:
        s_sends[k].wait_recv()
        s_total += s_near_recv[k]
    s_mid[group] = s_total
    s_mid_copies = []
    for k, o in enumerate(FAR):
        copy = remote(s_mid.at[group], s_mid.at[group], s_mid_s.at[k], s_mid_r.at[k], at(o))
        copy.start()
        s_mid_copies.append(copy)

    def eliminate(k, c):
        m = aug[...]
        pivot_row = aug[pl.ds(k, 1), :]
        column = jnp.sum(jnp.where(lane == k, m, 0.0), axis=1, keepdims=True)
        pivot = jnp.sum(jnp.where(lane[:1] == k, pivot_row, 0.0), axis=1, keepdims=True)
        factor = jnp.where(row[:, :1] > k, column, 0.0)
        aug[...] = m - factor * (pivot_row / pivot)
        return c

    lax.fori_loop(0, RANK, eliminate, 0)
    m = aug[...]
    diagonal = jnp.sum(jnp.where(lane == row, m, 0.0), axis=1, keepdims=True)
    l_inverse = (m / jnp.sqrt(diagonal))[:, RANK:]

    @pl.loop(0, 2 * WIN)
    def _(b):
        block = p_full[lax.rem(b, 2), b // 2].astype(F32)
        p_cols[b] = jnp.concatenate([block, block], axis=0).T.astype(BF16)

    for copy in s_mid_copies:
        copy.wait_recv()
    s_chunk = s_mid[0]
    for g in range(1, GROUPS):
        s_chunk += s_mid[g]
    s_full[core, mine] = s_chunk
    s_gathers, s_passes = [], []
    for k, e in enumerate(NEAR):
        copy = remote(
            s_full.at[core, mine], s_full.at[core, mine], s_gather_s.at[k], s_gather_r.at[k], at(-e)
        )
        copy.start()
        s_gathers.append(copy)

    def s_hand_on(k, j):
        copy = remote(s_full.at[core, j], s_full.at[core, j], s_pass_s.at[k], s_pass_r.at[k], partner)
        copy.start()
        s_passes.append(copy)

    s_hand_on(len(NEAR), mine)

    from_peers[tensor] = part[pl.ds(pl.multiple_of(tensor * ROWS, ROWS), ROWS), :]
    for copy in peer_copies:
        copy.wait_recv()

    @pl.loop(0, D_WIN // 512)
    def _(i):
        columns = pl.ds(pl.multiple_of(i * 512, 512), 512)
        acc = from_peers[0, :, columns].astype(F32)
        for t in range(1, PEERS):
            acc += from_peers[t, :, columns].astype(F32)
        summed[:, columns] = acc.astype(BF16)

    store_summed = pltpu.make_async_copy(summed, summed_hbm, store_sems.at[0])
    store_summed.start()

    for k in order:
        j = gather_from(k)
        remote(
            s_full.at[core, j], s_full.at[core, j], s_gather_s.at[k], s_gather_r.at[k], at(NEAR[k])
        ).wait_recv()
        s_hand_on(k, j)
    for k in [len(NEAR)] + order:
        j = mine if k == len(NEAR) else gather_from(k)
        remote(
            s_full.at[other, j], s_full.at[other, j], s_pass_s.at[k], s_pass_r.at[k], partner
        ).wait_recv()

    highest = lax.Precision.HIGHEST
    s_whole = jnp.concatenate([s_full[0].reshape(RANK, half_cols), s_full[1].reshape(RANK, half_cols)], axis=1)
    q_t = dot(l_inverse, s_whole, ((1,), (0,)), highest)
    q_out[...] = q_t
    store_q = pltpu.make_async_copy(q_out, q_out_hbm, store_sems.at[1])
    store_q.start()
    right = dot(l_inverse, q_t, ((0,), (0,)), highest) * (1.0 / (2 * CHIPS))
    right_high, right_low = halves(right)
    right_parts = jnp.concatenate([right_high, right_low], axis=0)

    def store_error(b):
        rows = pl.ds(b * BLK, BLK)
        return pltpu.make_async_copy(error.at[rows], error_hbm.at[rows], store_sems.at[2 + b])

    @pl.loop(0, 2 * WIN)
    def _(b):
        rows = pl.ds(pl.multiple_of(b * BLK, BLK), BLK)
        error[rows, :] = (gradient[b] - dot(p_cols[b], right_parts, ((1,), (0,)))).astype(BF16)
        store_error(b).start()

    for copy in [pair] + sends + mid_copies + gathers + passes + peer_copies:
        copy.wait_send()
    for copy in [s_pair_copy] + s_sends + s_mid_copies + s_gathers + s_passes:
        copy.wait_send()
    store_summed.wait()
    store_q.wait()

    @pl.loop(0, 2 * WIN)
    def _(b):
        store_error(b).wait()


def shards(activations, out_grads, query_weight, carried_q):
    any_space = pl.BlockSpec(memory_space=pl.ANY)
    dma = pltpu.SemaphoreType.DMA
    near = len(NEAR)
    far = len(FAR)
    summed, q_summed, error = pl.pallas_call(
        kernel,
        out_shape=(
            jax.ShapeDtypeStruct((ROWS, D_WIN), BF16),
            jax.ShapeDtypeStruct((RANK, COLS), F32),
            jax.ShapeDtypeStruct((D_WIN, COLS), BF16),
        ),
        in_specs=[any_space] * 4,
        out_specs=(any_space,) * 3,
        scratch_shapes=[
            pltpu.VMEM((2 * WIN, TOK, BLK), BF16),
            pltpu.VMEM((TOK, COLS), BF16),
            pltpu.VMEM((D_WIN, COLS), BF16),
            pltpu.VMEM((RANK, COLS), F32),
            pltpu.VMEM((2 * WIN, BLK, COLS), F32),
            pltpu.VMEM((TOK, D_WIN), BF16),
            pltpu.VMEM((PEERS, ROWS, D_WIN), BF16),
            pltpu.VMEM((ROWS, D_WIN), BF16),
            pltpu.VMEM((WIN, RANK, BLK), BF16),
            pltpu.VMEM((WIN, RANK, BLK), F32),
            pltpu.VMEM((WIN, RANK, BLK), BF16),
            pltpu.VMEM((near, RANK, BLK), BF16),
            pltpu.VMEM((near, RANK, BLK), BF16),
            pltpu.VMEM((GROUPS, RANK, BLK), BF16),
            pltpu.VMEM((2, WIN, RANK, BLK), BF16),
            pltpu.VMEM((2 * WIN, BLK, 2 * RANK), BF16),
            pltpu.VMEM((RANK, 2 * RANK), F32),
            pltpu.VMEM((2, RANK, COLS // 2), F32),
            pltpu.VMEM((RANK, COLS // 2), F32),
            pltpu.VMEM((RANK, COLS // 2), F32),
            pltpu.VMEM((near, RANK // WIN, COLS // 2), F32),
            pltpu.VMEM((GROUPS, RANK // WIN, COLS // 2), F32),
            pltpu.VMEM((2, WIN, RANK // WIN, COLS // 2), F32),
            pltpu.VMEM((RANK, COLS), F32),
            pltpu.VMEM((D_WIN, COLS), BF16),
            dma((3,)), dma((2 * WIN,)), dma((2 + 2 * WIN,)),
            dma((PEERS - 1,)), dma((PEERS - 1,)),
            dma((2,)),
            dma((near,)), dma((near,)),
            dma((far,)), dma((far,)),
            dma((near,)), dma((near,)),
            dma((near + 1,)), dma((near + 1,)),
            dma((2,)),
            dma((near,)), dma((near,)),
            dma((far,)), dma((far,)),
            dma((near,)), dma((near,)),
            dma((near + 1,)), dma((near + 1,)),
        ],
        compiler_params=pltpu.CompilerParams(
            collective_id=0, has_side_effects=True, vmem_limit_bytes=48 * 1024 * 1024
        ),
        name="powersgd",
    )(activations, out_grads, query_weight, carried_q.T)
    return summed, q_summed.T, error[None]


def solution(mesh):
    in_specs = (P("replica", None), P("replica", "tensor"), P(None, "tensor"), P("tensor", None))
    out_specs = (P(("replica", "tensor"), None), P("tensor", None), P("replica", None, "tensor"))
    return jax.shard_map(shards, mesh=mesh, in_specs=in_specs, out_specs=out_specs, check_vma=False)
```

```python
import jax
import jax.numpy as jnp
from jax import lax
from jax.experimental import pallas as pl
from jax.experimental.pallas import tpu as pltpu
from jax.sharding import PartitionSpec as P

MESH = pl.DeviceIdType.MESH
F32 = jnp.float32
BF16 = jnp.bfloat16

D_WIN = 4096
COLS = 256
TOK = 256
RANK = 64
CHIPS = 32
WIN = 8
GROUPS = CHIPS // WIN
PEERS = 16
BLK = D_WIN // (2 * WIN)
ROWS = TOK // PEERS

HALF = RANK // 2
S_WIN = 4
S_ROWS = RANK // (2 * S_WIN)

NEAR = (-4, 3, -3, 2, -2, 1, -1)
FAR = (16, 8, 24)
S_NEAR = (-2, 1, -1)
S_FAR = (16, 12, 20, 8, 24, 4, 28)


def dot(a, b, dims, precision=None):
    return lax.dot_general(a, b, (dims, ((), ())), precision=precision, preferred_element_type=F32)


def halves(x):
    high = x.astype(BF16)
    return high, (x - high.astype(F32)).astype(BF16)


def kernel(
    act_hbm, grad_hbm, weight_hbm, q_hbm,
    summed_hbm, q_out_hbm, error_hbm,
    act, og, weight, carried, gradient, part, from_peers, summed,
    p_send, p_acc, p_pair, near_send, near_recv, mid, p_full, p_cols, z, gram, aug, apply_ref,
    s_all, s_near_recv, s_mid, s_full, right_parts, q_out, error,
    load_sems, act_sems, store_sems, peer_send, peer_recv,
    pair_s, pair_r, near_s, near_r, mid_s, mid_r, gather_s, gather_r, pass_s, pass_r,
    s_near_s, s_near_r, s_mid_s, s_mid_r, s_gather_s, s_gather_r,
):
    replica = lax.axis_index("replica")
    tensor = lax.axis_index("tensor")
    chip = replica // 2
    core = lax.rem(replica, 2)
    other = 1 - core
    sign = 1 - 2 * core
    mine = lax.rem(chip, WIN)
    group = chip // WIN

    def chip_at(offset):
        return lax.rem(chip + offset + CHIPS, CHIPS)

    def at(offset, on=None):
        return (chip_at(offset) * 2 + (core if on is None else on), tensor)

    partner = at(0, other)

    def peer(offset):
        return (replica, lax.rem(tensor + offset, PEERS))

    def remote(src, dst, send, recv, device):
        return pltpu.make_async_remote_copy(
            src_ref=src, dst_ref=dst, send_sem=send, recv_sem=recv, device_id=device, device_id_type=MESH
        )

    load_og = pltpu.make_async_copy(grad_hbm, og, load_sems.at[0])
    load_q = pltpu.make_async_copy(q_hbm, carried, load_sems.at[1])
    load_weight = pltpu.make_async_copy(weight_hbm, weight, load_sems.at[2])
    load_og.start()
    load_q.start()

    def load_act(index):
        half, j = index // WIN, lax.rem(index, WIN)
        b = 2 * j + lax.rem(half + other, 2)
        return pltpu.make_async_copy(act_hbm.at[:, pl.ds(b * BLK, BLK)], act.at[b], act_sems.at[index])

    @pl.loop(0, 2 * WIN)
    def _(i):
        load_act(i).start()

    barrier = pltpu.get_barrier_semaphore()
    friends = [at(o) for o in (16, 12, -12, 8, -8, 4, -4, 3, -3, 2, -2, 1, -1)]
    friends += [at(o, other) for o in (2, -2, 1, -1)] + [partner]
    friends += [peer(o) for o in range(1, PEERS)]
    for friend in friends:
        pl.semaphore_signal(barrier, inc=1, device_id=friend, device_id_type=MESH)

    load_weight.start()

    load_og.wait()
    load_q.wait()
    q_high, q_low = halves(carried[...])
    y2 = dot(jnp.concatenate([q_high, q_low], axis=0), og[...], ((1,), (1,)))
    y_high, y_low = halves(y2[:RANK] + y2[RANK:])
    y_parts = jnp.concatenate([y_high, y_low], axis=0)

    def p_blocks(first, start, half, out):
        for j in range(first, first + WIN // 2):
            load_act(start + j).wait()
        for j in range(first, first + WIN // 2):
            both = dot(y_parts, act[2 * j + half], ((1,), (0,)))
            block = (both[:RANK] + both[RANK:]).astype(out.dtype)
            out[0, j] = block[:HALF]
            out[1, j] = block[HALF:]

    for start, half, out in ((0, other, p_send), (WIN, core, p_acc)):
        for first in (0, WIN // 2):
            p_blocks(first, start, half, out)

    pl.semaphore_wait(barrier, len(friends))

    pairs = []
    for h in range(2):
        copy = remote(p_send.at[h], p_pair.at[h], pair_s.at[h], pair_r.at[h], partner)
        copy.start()
        pairs.append(copy)

    sends = []
    for h in range(2):
        pairs[h].wait_recv()
        for k, e in enumerate(NEAR):
            j = lax.rem(chip_at(sign * e), WIN)
            near_send[h, k] = (p_acc[h, j] + p_pair[h, j].astype(F32)).astype(BF16)
            copy = remote(near_send.at[h, k], near_recv.at[h, k], near_s.at[h, k], near_r.at[h, k], at(sign * e))
            copy.start()
            sends.append(copy)

    load_weight.wait()

    @pl.loop(0, D_WIN // COLS, unroll=4)
    def _(b):
        rows = pl.ds(pl.multiple_of(b * COLS, COLS), COLS)
        part[:, rows] = dot(og[...], weight[rows, :], ((1,), (1,))).astype(BF16)

    peer_copies = []
    for o in range(1, PEERS):
        to = lax.rem(tensor + o, PEERS)
        copy = remote(
            part.at[pl.ds(pl.multiple_of(to * ROWS, ROWS), ROWS)], from_peers.at[tensor],
            peer_send.at[o - 1], peer_recv.at[o - 1], peer(o),
        )
        copy.start()
        peer_copies.append(copy)

    order = list(reversed(range(len(NEAR))))
    mid_copies = []
    for h in range(2):
        total = p_acc[h, mine] + p_pair[h, mine].astype(F32)
        for k in order:
            sends[h * len(NEAR) + k].wait_recv()
            total += near_recv[h, k].astype(F32)
        mid[h, group] = total.astype(BF16)
        for k, o in enumerate(FAR):
            copy = remote(mid.at[h, group], mid.at[h, group], mid_s.at[h, k], mid_r.at[h, k], at(o))
            copy.start()
            mid_copies.append(copy)

    @pl.loop(0, D_WIN // BLK, unroll=4)
    def _(b):
        gradient[b] = dot(act[b], og[...], ((0,), (0,)))

    def gather_from(k):
        return lax.rem(chip_at(sign * NEAR[k]), WIN)

    gathers, passes = [], []

    def hand_on(h, k, j):
        copy = remote(p_full.at[core, j, h], p_full.at[core, j, h], pass_s.at[h, k], pass_r.at[h, k], partner)
        copy.start()
        passes.append(copy)

    for h in range(2):
        for k in range(len(FAR)):
            mid_copies[h * len(FAR) + k].wait_recv()
        chunk = mid[h, 0].astype(F32)
        for g in range(1, GROUPS):
            chunk += mid[h, g].astype(F32)
        p_full[core, mine, h] = chunk.astype(BF16)
        for k, e in enumerate(NEAR):
            copy = remote(
                p_full.at[core, mine, h], p_full.at[core, mine, h], gather_s.at[h, k], gather_r.at[h, k],
                at(-sign * e),
            )
            copy.start()
            gathers.append(copy)
        hand_on(h, len(NEAR), mine)

    def p_whole(half, j):
        return p_full[half, j].reshape(RANK, BLK)

    def z_gram(half, j):
        block = p_whole(half, j)
        z[...] += dot(block, act[2 * j + half], ((1,), (1,)))
        gram[...] += dot(block, block, ((1,), (1,)))

    z[...] = jnp.zeros_like(z)
    gram[...] = jnp.zeros_like(gram)
    for h in range(2):
        for k in order:
            j = gather_from(k)
            remote(
                p_full.at[core, j, h], p_full.at[core, j, h], gather_s.at[h, k], gather_r.at[h, k],
                at(sign * NEAR[k]),
            ).wait_recv()
            hand_on(h, k, j)
    for k in [len(NEAR)] + order:
        j = mine if k == len(NEAR) else gather_from(k)
        z_gram(core, j)
    for k in [len(NEAR)] + order:
        j = mine if k == len(NEAR) else lax.rem(chip_at(-sign * NEAR[k]), WIN)
        for h in range(2):
            remote(
                p_full.at[other, j, h], p_full.at[other, j, h], pass_s.at[h, k], pass_r.at[h, k], partner
            ).wait_recv()
        z_gram(other, j)

    z_high, z_low = halves(z[...])
    s2 = dot(jnp.concatenate([z_high, z_low], axis=0), og[...], ((1,), (0,)))
    s_all[...] = s2[:RANK] + s2[RANK:]

    s_targets = [(e, core) for e in S_NEAR] + [(e, other) for e in S_NEAR] + [(0, other)]

    def s_chunk_of(chip_index, on):
        return 2 * lax.rem(chip_index, S_WIN) + on

    def s_rows(i):
        return pl.ds(pl.multiple_of(i * S_ROWS, S_ROWS), S_ROWS)

    s_mine = s_chunk_of(chip, core)
    s_group = chip // S_WIN
    s_sends = []
    for k, (e, on) in enumerate(s_targets):
        copy = remote(
            s_all.at[s_rows(s_chunk_of(chip_at(sign * e), on))], s_near_recv.at[k],
            s_near_s.at[k], s_near_r.at[k], at(sign * e, on),
        )
        copy.start()
        s_sends.append(copy)

    lane = lax.broadcasted_iota(jnp.int32, (RANK, 2 * RANK), 1)
    row = lax.broadcasted_iota(jnp.int32, (RANK, 2 * RANK), 0)
    aug[...] = jnp.concatenate([gram[...], (lane == row)[:, :RANK].astype(F32)], axis=1)

    @pl.loop(0, 2 * WIN, unroll=4)
    def _(b):
        block = p_whole(lax.rem(b, 2), b // 2)
        p_cols[b] = jnp.concatenate([block, block], axis=0).T

    s_total = s_all[s_rows(s_mine)]
    for k in reversed(range(len(s_targets))):
        s_sends[k].wait_recv()
        s_total += s_near_recv[k]
    s_mid[s_group] = s_total
    s_mid_copies = []
    for k, o in enumerate(S_FAR):
        copy = remote(s_mid.at[s_group], s_mid.at[s_group], s_mid_s.at[k], s_mid_r.at[k], at(o))
        copy.start()
        s_mid_copies.append(copy)

    def eliminate(k, c):
        m = aug[...]
        pivot_row = aug[pl.ds(k, 1), :]
        column = jnp.sum(jnp.where(lane == k, m, 0.0), axis=1, keepdims=True)
        pivot = jnp.sum(jnp.where(lane[:1] == k, pivot_row, 0.0), axis=1, keepdims=True)
        factor = jnp.where(row[:, :1] > k, column, 0.0)
        aug[...] = m - factor * (pivot_row / pivot)
        return c

    lax.fori_loop(0, RANK, eliminate, 0)
    m = aug[...]
    diagonal = jnp.sum(jnp.where(lane == row, m, 0.0), axis=1, keepdims=True)
    l_inverse = (m / jnp.sqrt(diagonal))[:, RANK:]
    highest = lax.Precision.HIGHEST
    apply = jnp.concatenate(
        [l_inverse, dot(l_inverse, l_inverse, ((0,), (0,)), highest) * (1.0 / (2 * CHIPS))], axis=0
    )

    apply_ref[...] = apply
    for copy in s_mid_copies:
        copy.wait_recv()
    s_chunk = s_mid[0]
    for g in range(1, CHIPS // S_WIN):
        s_chunk += s_mid[g]
    s_full[s_mine] = s_chunk
    s_gathers = []
    for k, (e, on) in enumerate(s_targets):
        copy = remote(
            s_full.at[s_mine], s_full.at[s_mine], s_gather_s.at[k], s_gather_r.at[k], at(-sign * e, on)
        )
        copy.start()
        s_gathers.append(copy)
    from_peers[tensor] = part[pl.ds(pl.multiple_of(tensor * ROWS, ROWS), ROWS), :]
    for copy in peer_copies:
        copy.wait_recv()

    @pl.loop(0, D_WIN // 512, unroll=2)
    def _(i):
        columns = pl.ds(pl.multiple_of(i * 512, 512), 512)
        acc = from_peers[0, :, columns].astype(F32)
        for t in range(1, PEERS):
            acc += from_peers[t, :, columns].astype(F32)
        summed[:, columns] = acc.astype(BF16)

    store_summed = pltpu.make_async_copy(summed, summed_hbm, store_sems.at[0])
    store_summed.start()

    for k in reversed(range(len(s_targets))):
        e, on = s_targets[k]
        toward = sign * e if k < len(S_NEAR) else -sign * e
        i = s_chunk_of(chip_at(toward), on)
        remote(
            s_full.at[i], s_full.at[i], s_gather_s.at[k], s_gather_r.at[k], at(toward, on)
        ).wait_recv()

    both = dot(apply_ref[...], s_full[...].reshape(RANK, COLS), ((1,), (0,)), highest)
    right_high, right_low = halves(both[RANK:])
    right_parts[...] = jnp.concatenate([right_high, right_low], axis=0)

    q_out[...] = both[:RANK]
    store_q = pltpu.make_async_copy(q_out, q_out_hbm, store_sems.at[1])
    store_q.start()

    def store_error(g):
        rows = pl.ds(g * 4 * BLK, 4 * BLK)
        return pltpu.make_async_copy(error.at[rows], error_hbm.at[rows], store_sems.at[2 + g])

    for g in range(WIN // 2):
        for b in range(4 * g, 4 * g + 4):
            product = dot(p_cols[b], right_parts[...], ((1,), (0,)))
            error[pl.ds(b * BLK, BLK), :] = (gradient[b] - product).astype(BF16)
        store_error(g).start()

    for copy in pairs + sends + mid_copies + gathers + passes + peer_copies + s_sends + s_mid_copies + s_gathers:
        copy.wait_send()
    store_summed.wait()
    store_q.wait()

    for g in range(WIN // 2):
        store_error(g).wait()


def shards(activations, out_grads, query_weight, carried_q):
    in_hbm = pl.BlockSpec(memory_space=pltpu.HBM)
    dma = pltpu.SemaphoreType.DMA
    near, far, s_near, s_far = len(NEAR), len(FAR), 2 * len(S_NEAR) + 1, len(S_FAR)
    summed, q_summed, error = pl.pallas_call(
        kernel,
        out_shape=(
            jax.ShapeDtypeStruct((ROWS, D_WIN), BF16),
            jax.ShapeDtypeStruct((RANK, COLS), F32),
            jax.ShapeDtypeStruct((D_WIN, COLS), BF16),
        ),
        in_specs=[in_hbm] * 4,
        out_specs=(pl.BlockSpec(memory_space=pl.ANY),) * 3,
        scratch_shapes=[
            pltpu.VMEM((2 * WIN, TOK, BLK), BF16),
            pltpu.VMEM((TOK, COLS), BF16),
            pltpu.VMEM((D_WIN, COLS), BF16),
            pltpu.VMEM((RANK, COLS), F32),
            pltpu.VMEM((2 * WIN, BLK, COLS), F32),
            pltpu.VMEM((TOK, D_WIN), BF16),
            pltpu.VMEM((PEERS, ROWS, D_WIN), BF16),
            pltpu.VMEM((ROWS, D_WIN), BF16),
            pltpu.VMEM((2, WIN, HALF, BLK), BF16),
            pltpu.VMEM((2, WIN, HALF, BLK), F32),
            pltpu.VMEM((2, WIN, HALF, BLK), BF16),
            pltpu.VMEM((2, near, HALF, BLK), BF16),
            pltpu.VMEM((2, near, HALF, BLK), BF16),
            pltpu.VMEM((2, GROUPS, HALF, BLK), BF16),
            pltpu.VMEM((2, WIN, 2, HALF, BLK), BF16),
            pltpu.VMEM((2 * WIN, BLK, 2 * RANK), BF16),
            pltpu.VMEM((RANK, TOK), F32),
            pltpu.VMEM((RANK, RANK), F32),
            pltpu.VMEM((RANK, 2 * RANK), F32),
            pltpu.VMEM((2 * RANK, RANK), F32),
            pltpu.VMEM((RANK, COLS), F32),
            pltpu.VMEM((s_near, S_ROWS, COLS), F32),
            pltpu.VMEM((CHIPS // S_WIN, S_ROWS, COLS), F32),
            pltpu.VMEM((2 * S_WIN, S_ROWS, COLS), F32),
            pltpu.VMEM((2 * RANK, COLS), BF16),
            pltpu.VMEM((RANK, COLS), F32),
            pltpu.VMEM((D_WIN, COLS), BF16),
            dma((3,)), dma((2 * WIN,)), dma((2 + WIN // 2,)),
            dma((PEERS - 1,)), dma((PEERS - 1,)),
            dma((2,)), dma((2,)),
            dma((2, near)), dma((2, near)),
            dma((2, far)), dma((2, far)),
            dma((2, near)), dma((2, near)),
            dma((2, near + 1)), dma((2, near + 1)),
            dma((s_near,)), dma((s_near,)),
            dma((s_far,)), dma((s_far,)),
            dma((s_near,)), dma((s_near,)),
        ],
        compiler_params=pltpu.CompilerParams(
            collective_id=0, has_side_effects=True, vmem_limit_bytes=48 * 1024 * 1024
        ),
        name="powersgd",
    )(activations, out_grads, query_weight, carried_q.T)
    return summed, q_summed.T, error[None]


def solution(mesh):
    in_specs = (P("replica", None), P("replica", "tensor"), P(None, "tensor"), P("tensor", None))
    out_specs = (P(("replica", "tensor"), None), P("tensor", None), P("replica", None, "tensor"))
    return jax.shard_map(shards, mesh=mesh, in_specs=in_specs, out_specs=out_specs, check_vma=False)
```

```python
import jax
import jax.numpy as jnp
from jax import lax
from jax.experimental import pallas as pl
from jax.experimental.pallas import tpu as pltpu
from jax.sharding import PartitionSpec as P

MESH = pl.DeviceIdType.MESH
F32 = jnp.float32
BF16 = jnp.bfloat16

D_WIN = 4096
COLS = 256
TOK = 256
RANK = 64
CHIPS = 32
WIN = 8
GROUPS = CHIPS // WIN
PEERS = 16
BLK = D_WIN // (2 * WIN)
ROWS = TOK // PEERS

PIECES = 2
HALF = RANK // PIECES
S_WIN = 4
S_ROWS = RANK // (2 * S_WIN)

NEAR = (-4, 3, -3, 2, -2, 1, -1)
FAR = (16, 8, 24)
S_NEAR = (-2, 1, -1)
S_FAR = (16, 12, 20, 8, 24, 4, 28)


def dot(a, b, dims, precision=None):
    return lax.dot_general(a, b, (dims, ((), ())), precision=precision, preferred_element_type=F32)


def halves(x):
    high = x.astype(BF16)
    return high, (x - high.astype(F32)).astype(BF16)


def kernel(
    act_hbm, grad_hbm, weight_hbm, q_hbm,
    summed_out, q_sum_out, right_out, gradient_out, p_cols_out,
    act, og, weight, carried, gradient, part, from_peers, summed,
    p_send, p_acc, p_pair, near_send, near_recv, mid, p_full, p_cols, z, gram, aug, apply_ref,
    s_all, s_near_recv, s_mid, s_full, right_parts, q_out,
    load_sems, act_sems, store_sems, peer_send, peer_recv,
    pair_s, pair_r, near_s, near_r, mid_s, mid_r, gather_s, gather_r, pass_s, pass_r,
    s_near_s, s_near_r, s_mid_s, s_mid_r, s_gather_s, s_gather_r, far_ready,
):
    replica = lax.axis_index("replica")
    tensor = lax.axis_index("tensor")
    chip = replica // 2
    core = lax.rem(replica, 2)
    other = 1 - core
    sign = 1 - 2 * core
    mine = lax.rem(chip, WIN)
    group = chip // WIN

    def chip_at(offset):
        return lax.rem(chip + offset + CHIPS, CHIPS)

    def at(offset, on=None):
        return (chip_at(offset) * 2 + (core if on is None else on), tensor)

    partner = at(0, other)

    def peer(offset):
        return (replica, lax.rem(tensor + offset, PEERS))

    def remote(src, dst, send, recv, device):
        return pltpu.make_async_remote_copy(
            src_ref=src, dst_ref=dst, send_sem=send, recv_sem=recv, device_id=device, device_id_type=MESH
        )

    load_og = pltpu.make_async_copy(grad_hbm, og, load_sems.at[0])
    load_q = pltpu.make_async_copy(q_hbm, carried, load_sems.at[1])
    load_weight = pltpu.make_async_copy(weight_hbm, weight, load_sems.at[2])
    load_og.start()
    load_q.start()

    def load_act(index):
        half, j = index // WIN, lax.rem(index, WIN)
        b = 2 * j + lax.rem(half + other, 2)
        return pltpu.make_async_copy(act_hbm.at[:, pl.ds(b * BLK, BLK)], act.at[b], act_sems.at[index])

    @pl.loop(0, 2 * WIN)
    def _(i):
        load_act(i).start()

    barrier = pltpu.get_barrier_semaphore()
    friends = [at(o) for o in (8, -8, 4, -4, 3, -3, 2, -2, 1, -1)]
    friends += [at(o, other) for o in (2, -2, 1, -1)] + [partner]
    friends += [peer(o) for o in range(1, PEERS)]
    for friend in friends:
        pl.semaphore_signal(barrier, inc=1, device_id=friend, device_id_type=MESH)

    load_weight.start()

    load_og.wait()
    load_q.wait()
    q_high, q_low = halves(carried[...])
    y2 = dot(jnp.concatenate([q_high, q_low], axis=0), og[...], ((1,), (1,)))
    y_high, y_low = halves(y2[:RANK] + y2[RANK:])
    y_parts = jnp.concatenate([y_high, y_low], axis=0)

    def p_blocks(first, start, half, out):
        for j in range(first, first + WIN // 2):
            load_act(start + j).wait()
        for j in range(first, first + WIN // 2):
            both = dot(y_parts, act[2 * j + half], ((1,), (0,)))
            block = (both[:RANK] + both[RANK:]).astype(out.dtype)
            for h in range(PIECES):
                out[h, j] = block[h * HALF : (h + 1) * HALF]

    for start, half, out in ((0, other, p_send), (WIN, core, p_acc)):
        for first in (0, WIN // 2):
            p_blocks(first, start, half, out)

    pl.semaphore_wait(barrier, len(friends))
    for o in (8, -8):
        pl.semaphore_signal(far_ready, inc=1, device_id=at(o), device_id_type=MESH)

    pairs = []
    for h in range(PIECES):
        copy = remote(p_send.at[h], p_pair.at[h], pair_s.at[h], pair_r.at[h], partner)
        copy.start()
        pairs.append(copy)

    sends = []
    for h in range(PIECES):
        pairs[h].wait_recv()
        for k, e in enumerate(NEAR):
            j = lax.rem(chip_at(sign * e), WIN)
            near_send[h, k] = (p_acc[h, j] + p_pair[h, j].astype(F32)).astype(BF16)
            copy = remote(near_send.at[h, k], near_recv.at[h, k], near_s.at[h, k], near_r.at[h, k], at(sign * e))
            copy.start()
            sends.append(copy)

    load_weight.wait()

    @pl.loop(0, D_WIN // COLS, unroll=4)
    def _(b):
        rows = pl.ds(pl.multiple_of(b * COLS, COLS), COLS)
        part[:, rows] = dot(og[...], weight[rows, :], ((1,), (1,))).astype(BF16)

    peer_copies = []
    for o in range(1, PEERS):
        to = lax.rem(tensor + o, PEERS)
        copy = remote(
            part.at[pl.ds(pl.multiple_of(to * ROWS, ROWS), ROWS)], from_peers.at[tensor],
            peer_send.at[o - 1], peer_recv.at[o - 1], peer(o),
        )
        copy.start()
        peer_copies.append(copy)

    order = list(reversed(range(len(NEAR))))
    mid_copies = []
    for h in range(PIECES):
        if h == 0:
            pl.semaphore_wait(far_ready, 2)
        total = p_acc[h, mine] + p_pair[h, mine].astype(F32)
        for k in order:
            sends[h * len(NEAR) + k].wait_recv()
            total += near_recv[h, k].astype(F32)
        mid[h, group] = total.astype(BF16)
        for k, o in enumerate(FAR):
            copy = remote(mid.at[h, group], mid.at[h, group], mid_s.at[h, k], mid_r.at[h, k], at(o))
            copy.start()
            mid_copies.append(copy)

    @pl.loop(0, D_WIN // BLK, unroll=4)
    def _(b):
        gradient[b] = dot(act[b], og[...], ((0,), (0,)))

    store_gradient = pltpu.make_async_copy(gradient, gradient_out, store_sems.at[2])
    store_gradient.start()

    def gather_from(k):
        return lax.rem(chip_at(sign * NEAR[k]), WIN)

    gathers, passes = [], []

    def hand_on(h, k, j):
        copy = remote(p_full.at[core, j, h], p_full.at[core, j, h], pass_s.at[h, k], pass_r.at[h, k], partner)
        copy.start()
        passes.append(copy)

    for h in range(PIECES):
        for k in range(len(FAR)):
            mid_copies[h * len(FAR) + k].wait_recv()
        chunk = mid[h, 0].astype(F32)
        for g in range(1, GROUPS):
            chunk += mid[h, g].astype(F32)
        p_full[core, mine, h] = chunk.astype(BF16)
        for k, e in enumerate(NEAR):
            copy = remote(
                p_full.at[core, mine, h], p_full.at[core, mine, h], gather_s.at[h, k], gather_r.at[h, k],
                at(-sign * e),
            )
            copy.start()
            gathers.append(copy)
        hand_on(h, len(NEAR), mine)

    def p_whole(half, j):
        return p_full[half, j].reshape(RANK, BLK)

    def z_gram(half, j):
        block = p_whole(half, j)
        z[...] += dot(block, act[2 * j + half], ((1,), (1,)))
        gram[...] += dot(block, block, ((1,), (1,)))

    z[...] = jnp.zeros_like(z)
    gram[...] = jnp.zeros_like(gram)
    for h in range(PIECES):
        for k in order:
            j = gather_from(k)
            remote(
                p_full.at[core, j, h], p_full.at[core, j, h], gather_s.at[h, k], gather_r.at[h, k],
                at(sign * NEAR[k]),
            ).wait_recv()
            hand_on(h, k, j)
    for k in [len(NEAR)] + order:
        j = mine if k == len(NEAR) else gather_from(k)
        z_gram(core, j)
    for k in [len(NEAR)] + order:
        j = mine if k == len(NEAR) else lax.rem(chip_at(-sign * NEAR[k]), WIN)
        for h in range(PIECES):
            remote(
                p_full.at[other, j, h], p_full.at[other, j, h], pass_s.at[h, k], pass_r.at[h, k], partner
            ).wait_recv()
        z_gram(other, j)

    z_high, z_low = halves(z[...])
    s2 = dot(jnp.concatenate([z_high, z_low], axis=0), og[...], ((1,), (0,)))
    s_all[...] = s2[:RANK] + s2[RANK:]

    s_targets = [(e, core) for e in S_NEAR] + [(e, other) for e in S_NEAR] + [(0, other)]

    def s_chunk_of(chip_index, on):
        return 2 * lax.rem(chip_index, S_WIN) + on

    def s_rows(i):
        return pl.ds(pl.multiple_of(i * S_ROWS, S_ROWS), S_ROWS)

    s_mine = s_chunk_of(chip, core)
    s_group = chip // S_WIN
    s_sends = []
    for k, (e, on) in enumerate(s_targets):
        copy = remote(
            s_all.at[s_rows(s_chunk_of(chip_at(sign * e), on))], s_near_recv.at[k],
            s_near_s.at[k], s_near_r.at[k], at(sign * e, on),
        )
        copy.start()
        s_sends.append(copy)

    lane = lax.broadcasted_iota(jnp.int32, (RANK, 2 * RANK), 1)
    row = lax.broadcasted_iota(jnp.int32, (RANK, 2 * RANK), 0)
    aug[...] = jnp.concatenate([gram[...], (lane == row)[:, :RANK].astype(F32)], axis=1)

    @pl.loop(0, 2 * WIN, unroll=4)
    def _(b):
        block = p_whole(lax.rem(b, 2), b // 2)
        p_cols[b] = jnp.concatenate([block, block], axis=0).T

    store_p_cols = pltpu.make_async_copy(p_cols, p_cols_out, store_sems.at[3])
    store_p_cols.start()

    s_total = s_all[s_rows(s_mine)]
    for k in reversed(range(len(s_targets))):
        s_sends[k].wait_recv()
        s_total += s_near_recv[k]
    s_mid[s_group] = s_total
    s_mid_copies = []
    for k, o in enumerate(S_FAR):
        copy = remote(s_mid.at[s_group], s_mid.at[s_group], s_mid_s.at[k], s_mid_r.at[k], at(o))
        copy.start()
        s_mid_copies.append(copy)

    def eliminate(k, c):
        m = aug[...]
        pivot_row = aug[pl.ds(k, 1), :]
        column = jnp.sum(jnp.where(lane == k, m, 0.0), axis=1, keepdims=True)
        pivot = jnp.sum(jnp.where(lane[:1] == k, pivot_row, 0.0), axis=1, keepdims=True)
        factor = jnp.where(row[:, :1] > k, column, 0.0)
        aug[...] = m - factor * (pivot_row / pivot)
        return c

    lax.fori_loop(0, RANK, eliminate, 0)
    m = aug[...]
    diagonal = jnp.sum(jnp.where(lane == row, m, 0.0), axis=1, keepdims=True)
    l_inverse = (m / jnp.sqrt(diagonal))[:, RANK:]
    highest = lax.Precision.HIGHEST
    apply = jnp.concatenate(
        [l_inverse, dot(l_inverse, l_inverse, ((0,), (0,)), highest) * (1.0 / (2 * CHIPS))], axis=0
    )

    apply_ref[...] = apply
    for copy in s_mid_copies:
        copy.wait_recv()
    s_chunk = s_mid[0]
    for g in range(1, CHIPS // S_WIN):
        s_chunk += s_mid[g]
    s_full[s_mine] = s_chunk
    s_gathers = []
    for k, (e, on) in enumerate(s_targets):
        copy = remote(
            s_full.at[s_mine], s_full.at[s_mine], s_gather_s.at[k], s_gather_r.at[k], at(-sign * e, on)
        )
        copy.start()
        s_gathers.append(copy)
    from_peers[tensor] = part[pl.ds(pl.multiple_of(tensor * ROWS, ROWS), ROWS), :]
    for copy in peer_copies:
        copy.wait_recv()

    @pl.loop(0, D_WIN // 512, unroll=2)
    def _(i):
        columns = pl.ds(pl.multiple_of(i * 512, 512), 512)
        acc = from_peers[0, :, columns].astype(F32)
        for t in range(1, PEERS):
            acc += from_peers[t, :, columns].astype(F32)
        summed[:, columns] = acc.astype(BF16)

    store_summed = pltpu.make_async_copy(summed, summed_out, store_sems.at[0])
    store_summed.start()

    for k in reversed(range(len(s_targets))):
        e, on = s_targets[k]
        toward = sign * e if k < len(S_NEAR) else -sign * e
        i = s_chunk_of(chip_at(toward), on)
        remote(
            s_full.at[i], s_full.at[i], s_gather_s.at[k], s_gather_r.at[k], at(toward, on)
        ).wait_recv()

    both = dot(apply_ref[...], s_full[...].reshape(RANK, COLS), ((1,), (0,)), highest)
    right_high, right_low = halves(both[RANK:])
    right_parts[...] = jnp.concatenate([right_high, right_low], axis=0)
    store_right = pltpu.make_async_copy(right_parts, right_out, store_sems.at[4])
    store_right.start()
    q_out[...] = both[:RANK]
    store_q = pltpu.make_async_copy(q_out, q_sum_out, store_sems.at[1])
    store_q.start()

    for copy in pairs + sends + mid_copies + gathers + passes + peer_copies + s_sends + s_mid_copies + s_gathers:
        copy.wait_send()
    for copy in (store_summed, store_gradient, store_p_cols, store_right, store_q):
        copy.wait()


def finish(
    summed, q_summed, right_parts, gradient, p_cols, summed_hbm, q_hbm, error_hbm, error, sems
):
    store_summed = pltpu.make_async_copy(summed, summed_hbm, sems.at[0])
    store_q = pltpu.make_async_copy(q_summed, q_hbm, sems.at[1])
    store_summed.start()
    store_q.start()
    stores = []
    for g in range(WIN // 2):
        for b in range(4 * g, 4 * g + 4):
            product = dot(p_cols[b], right_parts[...], ((1,), (0,)))
            error[pl.ds(b * BLK, BLK), :] = (gradient[b] - product).astype(BF16)
        rows = pl.ds(g * 4 * BLK, 4 * BLK)
        stores.append(pltpu.make_async_copy(error.at[rows], error_hbm.at[rows], sems.at[2 + g]))
        stores[-1].start()
    for copy in [store_summed, store_q] + stores:
        copy.wait()


def shards(activations, out_grads, query_weight, carried_q):
    in_hbm = pl.BlockSpec(memory_space=pltpu.HBM)
    dma = pltpu.SemaphoreType.DMA
    near, far, s_near, s_far = len(NEAR), len(FAR), 2 * len(S_NEAR) + 1, len(S_FAR)
    passed = (
        jax.ShapeDtypeStruct((ROWS, D_WIN), BF16),
        jax.ShapeDtypeStruct((RANK, COLS), F32),
        jax.ShapeDtypeStruct((2 * RANK, COLS), BF16),
        jax.ShapeDtypeStruct((2 * WIN, BLK, COLS), F32),
        jax.ShapeDtypeStruct((2 * WIN, BLK, 2 * RANK), BF16),
    )
    operands = (activations, out_grads, query_weight, carried_q.T)
    inputs = [pltpu.with_memory_space_constraint(x, pltpu.HBM) for x in operands]
    results = pl.pallas_call(
        kernel,
        out_shape=passed,
        in_specs=[in_hbm] * 4,
        out_specs=(pl.BlockSpec(memory_space=pl.ANY),) * len(passed),
        scratch_shapes=[
            pltpu.VMEM((2 * WIN, TOK, BLK), BF16),
            pltpu.VMEM((TOK, COLS), BF16),
            pltpu.VMEM((D_WIN, COLS), BF16),
            pltpu.VMEM((RANK, COLS), F32),
            pltpu.VMEM((2 * WIN, BLK, COLS), F32),
            pltpu.VMEM((TOK, D_WIN), BF16),
            pltpu.VMEM((PEERS, ROWS, D_WIN), BF16),
            pltpu.VMEM((ROWS, D_WIN), BF16),
            pltpu.VMEM((PIECES, WIN, HALF, BLK), BF16),
            pltpu.VMEM((PIECES, WIN, HALF, BLK), F32),
            pltpu.VMEM((PIECES, WIN, HALF, BLK), BF16),
            pltpu.VMEM((PIECES, near, HALF, BLK), BF16),
            pltpu.VMEM((PIECES, near, HALF, BLK), BF16),
            pltpu.VMEM((PIECES, GROUPS, HALF, BLK), BF16),
            pltpu.VMEM((2, WIN, PIECES, HALF, BLK), BF16),
            pltpu.VMEM((2 * WIN, BLK, 2 * RANK), BF16),
            pltpu.VMEM((RANK, TOK), F32),
            pltpu.VMEM((RANK, RANK), F32),
            pltpu.VMEM((RANK, 2 * RANK), F32),
            pltpu.VMEM((2 * RANK, RANK), F32),
            pltpu.VMEM((RANK, COLS), F32),
            pltpu.VMEM((s_near, S_ROWS, COLS), F32),
            pltpu.VMEM((CHIPS // S_WIN, S_ROWS, COLS), F32),
            pltpu.VMEM((2 * S_WIN, S_ROWS, COLS), F32),
            pltpu.VMEM((2 * RANK, COLS), BF16),
            pltpu.VMEM((RANK, COLS), F32),
            dma((3,)), dma((2 * WIN,)), dma((5,)),
            dma((PEERS - 1,)), dma((PEERS - 1,)),
            dma((PIECES,)), dma((PIECES,)),
            dma((PIECES, near)), dma((PIECES, near)),
            dma((PIECES, far)), dma((PIECES, far)),
            dma((PIECES, near)), dma((PIECES, near)),
            dma((PIECES, near + 1)), dma((PIECES, near + 1)),
            dma((s_near,)), dma((s_near,)),
            dma((s_far,)), dma((s_far,)),
            dma((s_near,)), dma((s_near,)),
            pltpu.SemaphoreType.REGULAR,
        ],
        compiler_params=pltpu.CompilerParams(
            collective_id=0, has_side_effects=True, vmem_limit_bytes=28 * 1024 * 1024
        ),
        name="powersgd",
    )(*inputs)
    summed, q_summed, error = pl.pallas_call(
        finish,
        out_shape=(passed[0], passed[1], jax.ShapeDtypeStruct((D_WIN, COLS), BF16)),
        in_specs=[pl.BlockSpec(memory_space=pltpu.VMEM)] * len(passed),
        out_specs=(pl.BlockSpec(memory_space=pl.ANY),) * 3,
        scratch_shapes=[pltpu.VMEM((D_WIN, COLS), BF16), dma((2 + WIN // 2,))],
        compiler_params=pltpu.CompilerParams(vmem_limit_bytes=24 * 1024 * 1024),
        name="finish",
    )(*results)
    return summed, q_summed.T, error[None]


def solution(mesh):
    in_specs = (P("replica", None), P("replica", "tensor"), P(None, "tensor"), P("tensor", None))
    out_specs = (P(("replica", "tensor"), None), P("tensor", None), P("replica", None, "tensor"))
    return jax.shard_map(shards, mesh=mesh, in_specs=in_specs, out_specs=out_specs, check_vma=False)
```

```python
import jax
import jax.numpy as jnp
from jax import lax
from jax.experimental import pallas as pl
from jax.experimental.pallas import tpu as pltpu
from jax.sharding import PartitionSpec as P

MESH = pl.DeviceIdType.MESH
F32 = jnp.float32
BF16 = jnp.bfloat16

D_WIN = 4096
COLS = 256
TOK = 256
RANK = 64
CHIPS = 32
WIN = 8
GROUPS = CHIPS // WIN
PEERS = 16
BLK = D_WIN // (2 * WIN)
ROWS = TOK // PEERS

PIECES = 2
HALF = RANK // PIECES
S_WIN = 4
S_ROWS = RANK // (2 * S_WIN)

NEAR = (-4, 3, -3, 2, -2, 1, -1)
FAR = (16, 8, 24)
S_NEAR = (-2, 1, -1)
S_FAR = (16, 12, 20, 8, 24, 4, 28)


def dot(a, b, dims, precision=None):
    return lax.dot_general(a, b, (dims, ((), ())), precision=precision, preferred_element_type=F32)


def halves(x):
    high = x.astype(BF16)
    return high, (x - high.astype(F32)).astype(BF16)


def kernel(
    act_hbm, grad_hbm, weight_hbm, q_hbm,
    summed_out, q_sum_out, right_out, gradient_out, p_cols_out,
    act, act_pair, og_pair, og, weight, carried, gradient, part, from_peers, summed,
    p_send, p_acc, p_pair, near_send, near_recv, mid, p_full, p_cols, z, gram, aug, apply_ref,
    s_all, s_near_recv, s_mid, s_full, right_parts, q_out,
    load_sems, act_sems, store_sems, peer_send, peer_recv,
    swap_s, swap_r, pair_s, pair_r, near_s, near_r, mid_s, mid_r, gather_s, gather_r, pass_s, pass_r,
    s_near_s, s_near_r, s_mid_s, s_mid_r, s_gather_s, s_gather_r, far_ready,
):
    replica = lax.axis_index("replica")
    tensor = lax.axis_index("tensor")
    chip = replica // 2
    core = lax.rem(replica, 2)
    other = 1 - core
    sign = 1 - 2 * core
    mine = lax.rem(chip, WIN)
    group = chip // WIN

    def chip_at(offset):
        return lax.rem(chip + offset + CHIPS, CHIPS)

    def at(offset, on=None):
        return (chip_at(offset) * 2 + (core if on is None else on), tensor)

    partner = at(0, other)

    def peer(offset):
        return (replica, lax.rem(tensor + offset, PEERS))

    def remote(src, dst, send, recv, device):
        return pltpu.make_async_remote_copy(
            src_ref=src, dst_ref=dst, send_sem=send, recv_sem=recv, device_id=device, device_id_type=MESH
        )

    load_og = pltpu.make_async_copy(grad_hbm, og, load_sems.at[0])
    load_q = pltpu.make_async_copy(q_hbm, carried, load_sems.at[1])
    load_weight = pltpu.make_async_copy(weight_hbm, weight, load_sems.at[2])
    load_og.start()
    load_q.start()

    def load_act(index):
        half, j = index // WIN, lax.rem(index, WIN)
        b = 2 * j + lax.rem(half + other, 2)
        return pltpu.make_async_copy(act_hbm.at[:, pl.ds(b * BLK, BLK)], act.at[lax.rem(half + other, 2), j], act_sems.at[index])

    @pl.loop(0, 2 * WIN)
    def _(i):
        load_act(i).start()

    barrier = pltpu.get_barrier_semaphore()
    friends = [at(o) for o in (8, -8, 4, -4, 3, -3, 2, -2, 1, -1)]
    friends += [at(o, other) for o in (2, -2, 1, -1)] + [partner]
    friends += [peer(o) for o in range(1, PEERS)]
    for friend in friends:
        pl.semaphore_signal(barrier, inc=1, device_id=friend, device_id_type=MESH)

    load_weight.start()

    load_og.wait()
    load_q.wait()
    q_high, q_low = halves(carried[...])
    y2 = dot(jnp.concatenate([q_high, q_low], axis=0), og[...], ((1,), (1,)))
    y_high, y_low = halves(y2[:RANK] + y2[RANK:])
    y_parts = jnp.concatenate([y_high, y_low], axis=0)

    def p_blocks(first, start, half, out):
        for j in range(first, first + WIN // 2):
            load_act(start + j).wait()
        for j in range(first, first + WIN // 2):
            both = dot(y_parts, act[half, j], ((1,), (0,)))
            block = (both[:RANK] + both[RANK:]).astype(out.dtype)
            for h in range(PIECES):
                out[h, j] = block[h * HALF : (h + 1) * HALF]

    for start, half, out in ((0, other, p_send), (WIN, core, p_acc)):
        for first in (0, WIN // 2):
            p_blocks(first, start, half, out)

    pl.semaphore_wait(barrier, len(friends))
    for o in (8, -8):
        pl.semaphore_signal(far_ready, inc=1, device_id=at(o), device_id_type=MESH)

    pairs = []
    for h in range(PIECES):
        copy = remote(p_send.at[h], p_pair.at[h], pair_s.at[h], pair_r.at[h], partner)
        copy.start()
        pairs.append(copy)

    sends = []
    for h in range(PIECES):
        pairs[h].wait_recv()
        for k, e in enumerate(NEAR):
            j = lax.rem(chip_at(sign * e), WIN)
            near_send[h, k] = (p_acc[h, j] + p_pair[h, j].astype(F32)).astype(BF16)
            copy = remote(near_send.at[h, k], near_recv.at[h, k], near_s.at[h, k], near_r.at[h, k], at(sign * e))
            copy.start()
            sends.append(copy)

    swaps = [
        remote(act.at[other], act_pair, swap_s.at[0], swap_r.at[0], partner),
        remote(og, og_pair, swap_s.at[1], swap_r.at[1], partner),
    ]
    for copy in swaps:
        copy.start()

    order = list(reversed(range(len(NEAR))))
    mid_copies = []
    for h in range(PIECES):
        if h == 0:
            pl.semaphore_wait(far_ready, 2)
        total = p_acc[h, mine] + p_pair[h, mine].astype(F32)
        for k in order:
            sends[h * len(NEAR) + k].wait_recv()
            total += near_recv[h, k].astype(F32)
        mid[h, group] = total.astype(BF16)
        for k, o in enumerate(FAR):
            copy = remote(mid.at[h, group], mid.at[h, group], mid_s.at[h, k], mid_r.at[h, k], at(o))
            copy.start()
            mid_copies.append(copy)

    load_weight.wait()

    @pl.loop(0, D_WIN // COLS, unroll=4)
    def _(b):
        rows = pl.ds(pl.multiple_of(b * COLS, COLS), COLS)
        part[:, rows] = dot(og[...], weight[rows, :], ((1,), (1,))).astype(BF16)

    peer_copies = []
    for o in range(1, PEERS):
        to = lax.rem(tensor + o, PEERS)
        copy = remote(
            part.at[pl.ds(pl.multiple_of(to * ROWS, ROWS), ROWS)], from_peers.at[tensor],
            peer_send.at[o - 1], peer_recv.at[o - 1], peer(o),
        )
        copy.start()
        peer_copies.append(copy)

    @pl.loop(0, D_WIN // BLK, unroll=4)
    def _(b):
        gradient[b] = dot(act[lax.rem(b, 2), b // 2], og[...], ((0,), (0,)))

    store_gradient = pltpu.make_async_copy(gradient, gradient_out, store_sems.at[2])
    store_gradient.start()

    def gather_from(k):
        return lax.rem(chip_at(sign * NEAR[k]), WIN)

    gathers, passes = [], []

    def hand_on(h, k, j):
        copy = remote(p_full.at[core, j, h], p_full.at[core, j, h], pass_s.at[h, k], pass_r.at[h, k], partner)
        copy.start()
        passes.append(copy)

    for h in range(PIECES):
        for k in range(len(FAR)):
            mid_copies[h * len(FAR) + k].wait_recv()
        chunk = mid[h, 0].astype(F32)
        for g in range(1, GROUPS):
            chunk += mid[h, g].astype(F32)
        p_full[core, mine, h] = chunk.astype(BF16)
        for k, e in enumerate(NEAR):
            copy = remote(
                p_full.at[core, mine, h], p_full.at[core, mine, h], gather_s.at[h, k], gather_r.at[h, k],
                at(-sign * e),
            )
            copy.start()
            gathers.append(copy)
        hand_on(h, len(NEAR), mine)

    def p_whole(half, j):
        return p_full[half, j].reshape(RANK, BLK)

    def add_gram(half, j):
        block = p_whole(half, j)
        gram[...] += dot(block, block, ((1,), (1,)))

    z[...] = jnp.zeros_like(z)
    gram[...] = jnp.zeros_like(gram)
    for copy in swaps:
        copy.wait_recv()
    for h in range(PIECES):
        for k in order:
            j = gather_from(k)
            remote(
                p_full.at[core, j, h], p_full.at[core, j, h], gather_s.at[h, k], gather_r.at[h, k],
                at(sign * NEAR[k]),
            ).wait_recv()
            hand_on(h, k, j)
    for j in range(WIN):
        block = p_whole(core, j)
        z[:, :TOK] += dot(block, act[core, j], ((1,), (1,)))
        z[:, TOK:] += dot(block, act_pair[j], ((1,), (1,)))

    z_high, z_low = halves(z[...])
    z_parts = jnp.concatenate([z_high, z_low], axis=0)
    s2 = dot(z_parts[:, :TOK], og[...], ((1,), (0,))) + dot(z_parts[:, TOK:], og_pair[...], ((1,), (0,)))
    s_all[...] = s2[:RANK] + s2[RANK:]

    s_targets = [(e, core) for e in S_NEAR] + [(e, other) for e in S_NEAR] + [(0, other)]

    def s_chunk_of(chip_index, on):
        return 2 * lax.rem(chip_index, S_WIN) + on

    def s_rows(i):
        return pl.ds(pl.multiple_of(i * S_ROWS, S_ROWS), S_ROWS)

    s_mine = s_chunk_of(chip, core)
    s_group = chip // S_WIN
    s_sends = []
    for k, (e, on) in enumerate(s_targets):
        copy = remote(
            s_all.at[s_rows(s_chunk_of(chip_at(sign * e), on))], s_near_recv.at[k],
            s_near_s.at[k], s_near_r.at[k], at(sign * e, on),
        )
        copy.start()
        s_sends.append(copy)

    for k in [len(NEAR)] + order:
        j = mine if k == len(NEAR) else lax.rem(chip_at(-sign * NEAR[k]), WIN)
        for h in range(PIECES):
            remote(
                p_full.at[other, j, h], p_full.at[other, j, h], pass_s.at[h, k], pass_r.at[h, k], partner
            ).wait_recv()

    for half in range(2):
        for j in range(WIN):
            add_gram(half, j)
    lane = lax.broadcasted_iota(jnp.int32, (RANK, 2 * RANK), 1)
    row = lax.broadcasted_iota(jnp.int32, (RANK, 2 * RANK), 0)
    aug[...] = jnp.concatenate([gram[...], (lane == row)[:, :RANK].astype(F32)], axis=1)

    @pl.loop(0, 2 * WIN, unroll=4)
    def _(b):
        block = p_whole(lax.rem(b, 2), b // 2)
        p_cols[b] = jnp.concatenate([block, block], axis=0).T

    store_p_cols = pltpu.make_async_copy(p_cols, p_cols_out, store_sems.at[3])
    store_p_cols.start()

    s_total = s_all[s_rows(s_mine)]
    for k in reversed(range(len(s_targets))):
        s_sends[k].wait_recv()
        s_total += s_near_recv[k]
    s_mid[s_group] = s_total
    s_mid_copies = []
    for k, o in enumerate(S_FAR):
        copy = remote(s_mid.at[s_group], s_mid.at[s_group], s_mid_s.at[k], s_mid_r.at[k], at(o))
        copy.start()
        s_mid_copies.append(copy)

    def eliminate(k, c):
        m = aug[...]
        pivot_row = aug[pl.ds(k, 1), :]
        column = jnp.sum(jnp.where(lane == k, m, 0.0), axis=1, keepdims=True)
        pivot = jnp.sum(jnp.where(lane[:1] == k, pivot_row, 0.0), axis=1, keepdims=True)
        factor = jnp.where(row[:, :1] > k, column, 0.0)
        aug[...] = m - factor * (pivot_row / pivot)
        return c

    lax.fori_loop(0, RANK, eliminate, 0)
    m = aug[...]
    diagonal = jnp.sum(jnp.where(lane == row, m, 0.0), axis=1, keepdims=True)
    l_inverse = (m / jnp.sqrt(diagonal))[:, RANK:]
    highest = lax.Precision.HIGHEST
    apply = jnp.concatenate(
        [l_inverse, dot(l_inverse, l_inverse, ((0,), (0,)), highest) * (1.0 / (2 * CHIPS))], axis=0
    )

    apply_ref[...] = apply
    for copy in s_mid_copies:
        copy.wait_recv()
    s_chunk = s_mid[0]
    for g in range(1, CHIPS // S_WIN):
        s_chunk += s_mid[g]
    s_full[s_mine] = s_chunk
    s_gathers = []
    for k, (e, on) in enumerate(s_targets):
        copy = remote(
            s_full.at[s_mine], s_full.at[s_mine], s_gather_s.at[k], s_gather_r.at[k], at(-sign * e, on)
        )
        copy.start()
        s_gathers.append(copy)
    from_peers[tensor] = part[pl.ds(pl.multiple_of(tensor * ROWS, ROWS), ROWS), :]
    for copy in peer_copies:
        copy.wait_recv()

    @pl.loop(0, D_WIN // 512, unroll=2)
    def _(i):
        columns = pl.ds(pl.multiple_of(i * 512, 512), 512)
        acc = from_peers[0, :, columns].astype(F32)
        for t in range(1, PEERS):
            acc += from_peers[t, :, columns].astype(F32)
        summed[:, columns] = acc.astype(BF16)

    store_summed = pltpu.make_async_copy(summed, summed_out, store_sems.at[0])
    store_summed.start()

    for k in reversed(range(len(s_targets))):
        e, on = s_targets[k]
        toward = sign * e if k < len(S_NEAR) else -sign * e
        i = s_chunk_of(chip_at(toward), on)
        remote(
            s_full.at[i], s_full.at[i], s_gather_s.at[k], s_gather_r.at[k], at(toward, on)
        ).wait_recv()

    both = dot(apply_ref[...], s_full[...].reshape(RANK, COLS), ((1,), (0,)), highest)
    right_high, right_low = halves(both[RANK:])
    right_parts[...] = jnp.concatenate([right_high, right_low], axis=0)
    store_right = pltpu.make_async_copy(right_parts, right_out, store_sems.at[4])
    store_right.start()
    q_out[...] = both[:RANK]
    store_q = pltpu.make_async_copy(q_out, q_sum_out, store_sems.at[1])
    store_q.start()

    for copy in swaps + pairs + sends + mid_copies + gathers + passes + peer_copies + s_sends + s_mid_copies + s_gathers:
        copy.wait_send()
    for copy in (store_summed, store_gradient, store_p_cols, store_right, store_q):
        copy.wait()


def finish(
    summed, q_summed, right_parts, gradient, p_cols, summed_hbm, q_hbm, error_hbm, error, sems
):
    store_summed = pltpu.make_async_copy(summed, summed_hbm, sems.at[0])
    store_q = pltpu.make_async_copy(q_summed, q_hbm, sems.at[1])
    store_summed.start()
    store_q.start()
    stores = []
    for g in range(WIN):
        for b in range(2 * g, 2 * g + 2):
            product = dot(p_cols[b], right_parts[...], ((1,), (0,)))
            error[pl.ds(b * BLK, BLK), :] = (gradient[b] - product).astype(BF16)
        rows = pl.ds(g * 2 * BLK, 2 * BLK)
        stores.append(pltpu.make_async_copy(error.at[rows], error_hbm.at[rows], sems.at[2 + g]))
        stores[-1].start()
    for copy in [store_summed, store_q] + stores:
        copy.wait()


def shards(activations, out_grads, query_weight, carried_q):
    in_hbm = pl.BlockSpec(memory_space=pltpu.HBM)
    dma = pltpu.SemaphoreType.DMA
    near, far, s_near, s_far = len(NEAR), len(FAR), 2 * len(S_NEAR) + 1, len(S_FAR)
    passed = (
        jax.ShapeDtypeStruct((ROWS, D_WIN), BF16),
        jax.ShapeDtypeStruct((RANK, COLS), F32),
        jax.ShapeDtypeStruct((2 * RANK, COLS), BF16),
        jax.ShapeDtypeStruct((2 * WIN, BLK, COLS), F32),
        jax.ShapeDtypeStruct((2 * WIN, BLK, 2 * RANK), BF16),
    )
    operands = (activations, out_grads, query_weight, carried_q.T)
    inputs = [pltpu.with_memory_space_constraint(x, pltpu.HBM) for x in operands]
    results = pl.pallas_call(
        kernel,
        out_shape=passed,
        in_specs=[in_hbm] * 4,
        out_specs=(pl.BlockSpec(memory_space=pl.ANY),) * len(passed),
        scratch_shapes=[
            pltpu.VMEM((2, WIN, TOK, BLK), BF16),
            pltpu.VMEM((WIN, TOK, BLK), BF16),
            pltpu.VMEM((TOK, COLS), BF16),
            pltpu.VMEM((TOK, COLS), BF16),
            pltpu.VMEM((D_WIN, COLS), BF16),
            pltpu.VMEM((RANK, COLS), F32),
            pltpu.VMEM((2 * WIN, BLK, COLS), F32),
            pltpu.VMEM((TOK, D_WIN), BF16),
            pltpu.VMEM((PEERS, ROWS, D_WIN), BF16),
            pltpu.VMEM((ROWS, D_WIN), BF16),
            pltpu.VMEM((PIECES, WIN, HALF, BLK), BF16),
            pltpu.VMEM((PIECES, WIN, HALF, BLK), F32),
            pltpu.VMEM((PIECES, WIN, HALF, BLK), BF16),
            pltpu.VMEM((PIECES, near, HALF, BLK), BF16),
            pltpu.VMEM((PIECES, near, HALF, BLK), BF16),
            pltpu.VMEM((PIECES, GROUPS, HALF, BLK), BF16),
            pltpu.VMEM((2, WIN, PIECES, HALF, BLK), BF16),
            pltpu.VMEM((2 * WIN, BLK, 2 * RANK), BF16),
            pltpu.VMEM((RANK, 2 * TOK), F32),
            pltpu.VMEM((RANK, RANK), F32),
            pltpu.VMEM((RANK, 2 * RANK), F32),
            pltpu.VMEM((2 * RANK, RANK), F32),
            pltpu.VMEM((RANK, COLS), F32),
            pltpu.VMEM((s_near, S_ROWS, COLS), F32),
            pltpu.VMEM((CHIPS // S_WIN, S_ROWS, COLS), F32),
            pltpu.VMEM((2 * S_WIN, S_ROWS, COLS), F32),
            pltpu.VMEM((2 * RANK, COLS), BF16),
            pltpu.VMEM((RANK, COLS), F32),
            dma((3,)), dma((2 * WIN,)), dma((5,)),
            dma((PEERS - 1,)), dma((PEERS - 1,)),
            dma((2,)), dma((2,)),
            dma((PIECES,)), dma((PIECES,)),
            dma((PIECES, near)), dma((PIECES, near)),
            dma((PIECES, far)), dma((PIECES, far)),
            dma((PIECES, near)), dma((PIECES, near)),
            dma((PIECES, near + 1)), dma((PIECES, near + 1)),
            dma((s_near,)), dma((s_near,)),
            dma((s_far,)), dma((s_far,)),
            dma((s_near,)), dma((s_near,)),
            pltpu.SemaphoreType.REGULAR,
        ],
        compiler_params=pltpu.CompilerParams(
            collective_id=0, has_side_effects=True, vmem_limit_bytes=28 * 1024 * 1024
        ),
        name="powersgd",
    )(*inputs)
    summed, q_summed, error = pl.pallas_call(
        finish,
        out_shape=(passed[0], passed[1], jax.ShapeDtypeStruct((D_WIN, COLS), BF16)),
        in_specs=[pl.BlockSpec(memory_space=pltpu.VMEM)] * len(passed),
        out_specs=(pl.BlockSpec(memory_space=pl.ANY),) * 3,
        scratch_shapes=[pltpu.VMEM((D_WIN, COLS), BF16), dma((2 + WIN,))],
        compiler_params=pltpu.CompilerParams(vmem_limit_bytes=24 * 1024 * 1024),
        name="finish",
    )(*results)
    return summed, q_summed.T, error[None]


def solution(mesh):
    in_specs = (P("replica", None), P("replica", "tensor"), P(None, "tensor"), P("tensor", None))
    out_specs = (P(("replica", "tensor"), None), P("tensor", None), P("replica", None, "tensor"))
    return jax.shard_map(shards, mesh=mesh, in_specs=in_specs, out_specs=out_specs, check_vma=False)
```

```python
import jax
import jax.numpy as jnp
from jax import lax
from jax.experimental import pallas as pl
from jax.experimental.pallas import tpu as pltpu
from jax.sharding import PartitionSpec as P

MESH = pl.DeviceIdType.MESH
F32 = jnp.float32
BF16 = jnp.bfloat16

D_WIN = 4096
COLS = 256
TOK = 256
RANK = 64
CHIPS = 32
WIN = 8
GROUPS = CHIPS // WIN
PEERS = 16
BLK = D_WIN // (2 * WIN)
ROWS = TOK // PEERS

PIECES = 2
HALF = RANK // PIECES
S_WIN = 4
S_ROWS = RANK // (2 * S_WIN)

NEAR = (-4, 3, -3, 2, -2, 1, -1)
FAR = (16, 8, 24)
S_NEAR = (-2, 1, -1)
S_FAR = (16, 12, 20, 8, 24, 4, 28)


def dot(a, b, dims, precision=None):
    return lax.dot_general(a, b, (dims, ((), ())), precision=precision, preferred_element_type=F32)


def halves(x):
    high = x.astype(BF16)
    return high, (x - high.astype(F32)).astype(BF16)


def kernel(
    act_hbm, grad_hbm, weight_hbm, q_hbm,
    summed_out, q_sum_out, right_out, gradient_out, p_cols_out,
    act, act_pair, og_pair, og, weight, carried, gradient, part, from_peers, summed,
    p_send, p_acc, p_pair, near_send, near_recv, mid, p_full, p_cols, z, gram, aug, apply_ref,
    s_all, s_near_recv, s_mid, s_full, right_parts, q_out,
    load_sems, act_sems, store_sems, peer_send, peer_recv,
    swap_s, swap_r, pair_s, pair_r, near_s, near_r, mid_s, mid_r, gather_s, gather_r, pass_s, pass_r,
    s_near_s, s_near_r, s_mid_s, s_mid_r, s_gather_s, s_gather_r, far_ready,
):
    replica = lax.axis_index("replica")
    tensor = lax.axis_index("tensor")
    chip = replica // 2
    core = lax.rem(replica, 2)
    other = 1 - core
    sign = 1 - 2 * core
    mine = lax.rem(chip, WIN)
    group = chip // WIN

    def chip_at(offset):
        return lax.rem(chip + offset + CHIPS, CHIPS)

    def at(offset, on=None):
        return (chip_at(offset) * 2 + (core if on is None else on), tensor)

    partner = at(0, other)

    def peer(offset):
        return (replica, lax.rem(tensor + offset, PEERS))

    def remote(src, dst, send, recv, device):
        return pltpu.make_async_remote_copy(
            src_ref=src, dst_ref=dst, send_sem=send, recv_sem=recv, device_id=device, device_id_type=MESH
        )

    load_og = pltpu.make_async_copy(grad_hbm, og, load_sems.at[0])
    load_q = pltpu.make_async_copy(q_hbm, carried, load_sems.at[1])
    load_weight = pltpu.make_async_copy(weight_hbm, weight, load_sems.at[2])
    load_og.start()
    load_q.start()

    def load_act(index):
        half, j = index // WIN, lax.rem(index, WIN)
        b = 2 * j + lax.rem(half + other, 2)
        return pltpu.make_async_copy(act_hbm.at[:, pl.ds(b * BLK, BLK)], act.at[lax.rem(half + other, 2), j], act_sems.at[index])

    @pl.loop(0, 2 * WIN)
    def _(i):
        load_act(i).start()

    barrier = pltpu.get_barrier_semaphore()
    friends = [at(o) for o in (8, -8, 4, -4, 3, -3, 2, -2, 1, -1)]
    friends += [at(o, other) for o in (2, -2, 1, -1)] + [partner]
    friends += [peer(o) for o in range(1, PEERS)]
    for friend in friends:
        pl.semaphore_signal(barrier, inc=1, device_id=friend, device_id_type=MESH)

    load_weight.start()

    load_og.wait()
    load_q.wait()
    q_high, q_low = halves(carried[...])
    y2 = dot(jnp.concatenate([q_high, q_low], axis=0), og[...], ((1,), (1,)))
    y_high, y_low = halves(y2[:RANK] + y2[RANK:])
    y_parts = jnp.concatenate([y_high, y_low], axis=0)

    def p_blocks(first, start, half, out):
        for j in range(first, first + WIN // 2):
            load_act(start + j).wait()
        for j in range(first, first + WIN // 2):
            both = dot(y_parts, act[half, j], ((1,), (0,)))
            block = (both[:RANK] + both[RANK:]).astype(out.dtype)
            for h in range(PIECES):
                out[h, j] = block[h * HALF : (h + 1) * HALF]

    for start, half, out in ((0, other, p_send), (WIN, core, p_acc)):
        for first in (0, WIN // 2):
            p_blocks(first, start, half, out)

    pl.semaphore_wait(barrier, len(friends))
    for o in (8, -8):
        pl.semaphore_signal(far_ready, inc=1, device_id=at(o), device_id_type=MESH)

    pairs = []
    for h in range(PIECES):
        copy = remote(p_send.at[h], p_pair.at[h], pair_s.at[h], pair_r.at[h], partner)
        copy.start()
        pairs.append(copy)

    sends = []
    for h in range(PIECES):
        pairs[h].wait_recv()
        for k, e in enumerate(NEAR):
            j = lax.rem(chip_at(sign * e), WIN)
            near_send[h, k] = (p_acc[h, j] + p_pair[h, j].astype(F32)).astype(BF16)
            copy = remote(near_send.at[h, k], near_recv.at[h, k], near_s.at[h, k], near_r.at[h, k], at(sign * e))
            copy.start()
            sends.append(copy)

    swaps = [
        remote(act.at[other], act_pair, swap_s.at[0], swap_r.at[0], partner),
        remote(og, og_pair, swap_s.at[1], swap_r.at[1], partner),
    ]
    for copy in swaps:
        copy.start()

    order = list(reversed(range(len(NEAR))))
    mid_copies = []
    for h in range(PIECES):
        if h == 0:
            pl.semaphore_wait(far_ready, 2)
        total = p_acc[h, mine] + p_pair[h, mine].astype(F32)
        for k in order:
            sends[h * len(NEAR) + k].wait_recv()
            total += near_recv[h, k].astype(F32)
        mid[h, group] = total.astype(BF16)
        for k, o in enumerate(FAR):
            copy = remote(mid.at[h, group], mid.at[h, group], mid_s.at[h, k], mid_r.at[h, k], at(o))
            copy.start()
            mid_copies.append(copy)

    load_weight.wait()

    @pl.loop(0, D_WIN // COLS, unroll=4)
    def _(b):
        rows = pl.ds(pl.multiple_of(b * COLS, COLS), COLS)
        part[:, rows] = dot(og[...], weight[rows, :], ((1,), (1,))).astype(BF16)

    peer_copies = []
    for o in range(1, PEERS):
        to = lax.rem(tensor + o, PEERS)
        copy = remote(
            part.at[pl.ds(pl.multiple_of(to * ROWS, ROWS), ROWS)], from_peers.at[tensor],
            peer_send.at[o - 1], peer_recv.at[o - 1], peer(o),
        )
        copy.start()
        peer_copies.append(copy)

    @pl.loop(0, D_WIN // BLK, unroll=4)
    def _(b):
        gradient[b] = dot(act[lax.rem(b, 2), b // 2], og[...], ((0,), (0,)))

    store_gradient = pltpu.make_async_copy(gradient, gradient_out, store_sems.at[2])
    store_gradient.start()

    def gather_from(k):
        return lax.rem(chip_at(sign * NEAR[k]), WIN)

    gathers, passes = [], []

    def hand_on(h, k, j):
        copy = remote(p_full.at[core, j, h], p_full.at[core, j, h], pass_s.at[h, k], pass_r.at[h, k], partner)
        copy.start()
        passes.append(copy)

    for h in range(PIECES):
        for k in range(len(FAR)):
            mid_copies[h * len(FAR) + k].wait_recv()
        chunk = mid[h, 0].astype(F32)
        for g in range(1, GROUPS):
            chunk += mid[h, g].astype(F32)
        p_full[core, mine, h] = chunk.astype(BF16)
        for k, e in enumerate(NEAR):
            copy = remote(
                p_full.at[core, mine, h], p_full.at[core, mine, h], gather_s.at[h, k], gather_r.at[h, k],
                at(-sign * e),
            )
            copy.start()
            gathers.append(copy)
        hand_on(h, len(NEAR), mine)

    def p_whole(half, j):
        return p_full[half, j].reshape(RANK, BLK)

    def add_gram(half, j):
        block = p_whole(half, j)
        gram[...] += dot(block, block, ((1,), (1,)))

    z[...] = jnp.zeros_like(z)
    gram[...] = jnp.zeros_like(gram)
    for copy in swaps:
        copy.wait_recv()
    for h in range(PIECES):
        for k in order:
            j = gather_from(k)
            remote(
                p_full.at[core, j, h], p_full.at[core, j, h], gather_s.at[h, k], gather_r.at[h, k],
                at(sign * NEAR[k]),
            ).wait_recv()
            hand_on(h, k, j)
    for j in range(WIN):
        block = p_whole(core, j)
        z[:, :TOK] += dot(block, act[core, j], ((1,), (1,)))
        z[:, TOK:] += dot(block, act_pair[j], ((1,), (1,)))

    z_high, z_low = halves(z[...])
    z_parts = jnp.concatenate([z_high, z_low], axis=0)
    s2 = dot(z_parts[:, :TOK], og[...], ((1,), (0,))) + dot(z_parts[:, TOK:], og_pair[...], ((1,), (0,)))
    s_all[...] = s2[:RANK] + s2[RANK:]

    s_targets = [(e, core) for e in S_NEAR] + [(e, other) for e in S_NEAR] + [(0, other)]

    def s_chunk_of(chip_index, on):
        return 2 * lax.rem(chip_index, S_WIN) + on

    def s_rows(i):
        return pl.ds(pl.multiple_of(i * S_ROWS, S_ROWS), S_ROWS)

    s_mine = s_chunk_of(chip, core)
    s_group = chip // S_WIN
    s_sends = []
    for k, (e, on) in enumerate(s_targets):
        copy = remote(
            s_all.at[s_rows(s_chunk_of(chip_at(sign * e), on))], s_near_recv.at[k],
            s_near_s.at[k], s_near_r.at[k], at(sign * e, on),
        )
        copy.start()
        s_sends.append(copy)

    for k in [len(NEAR)] + order:
        j = mine if k == len(NEAR) else lax.rem(chip_at(-sign * NEAR[k]), WIN)
        for h in range(PIECES):
            remote(
                p_full.at[other, j, h], p_full.at[other, j, h], pass_s.at[h, k], pass_r.at[h, k], partner
            ).wait_recv()

    for half in range(2):
        for j in range(WIN):
            add_gram(half, j)
    lane = lax.broadcasted_iota(jnp.int32, (RANK, 2 * RANK), 1)
    row = lax.broadcasted_iota(jnp.int32, (RANK, 2 * RANK), 0)
    aug[...] = jnp.concatenate([gram[...], (lane == row)[:, :RANK].astype(F32)], axis=1)

    @pl.loop(0, 2 * WIN, unroll=4)
    def _(b):
        block = p_whole(lax.rem(b, 2), b // 2)
        p_cols[b] = jnp.concatenate([block, block], axis=0).T

    store_p_cols = pltpu.make_async_copy(p_cols, p_cols_out, store_sems.at[3])
    store_p_cols.start()

    s_total = s_all[s_rows(s_mine)]
    for k in reversed(range(len(s_targets))):
        s_sends[k].wait_recv()
        s_total += s_near_recv[k]
    s_mid[s_group] = s_total
    s_mid_copies = []
    for k, o in enumerate(S_FAR):
        copy = remote(s_mid.at[s_group], s_mid.at[s_group], s_mid_s.at[k], s_mid_r.at[k], at(o))
        copy.start()
        s_mid_copies.append(copy)

    def eliminate(k, c):
        m = aug[...]
        pivot_row = aug[pl.ds(k, 1), :]
        column = jnp.sum(jnp.where(lane == k, m, 0.0), axis=1, keepdims=True)
        pivot = jnp.sum(jnp.where(lane[:1] == k, pivot_row, 0.0), axis=1, keepdims=True)
        factor = jnp.where(row[:, :1] > k, column, 0.0)
        aug[...] = m - factor * (pivot_row / pivot)
        return c

    lax.fori_loop(0, RANK, eliminate, 0)
    m = aug[...]
    diagonal = jnp.sum(jnp.where(lane == row, m, 0.0), axis=1, keepdims=True)
    l_inverse = (m / jnp.sqrt(diagonal))[:, RANK:]
    highest = lax.Precision.HIGHEST
    apply = jnp.concatenate(
        [l_inverse, dot(l_inverse, l_inverse, ((0,), (0,)), highest) * (1.0 / (2 * CHIPS))], axis=0
    )

    apply_ref[...] = apply
    from_peers[tensor] = part[pl.ds(pl.multiple_of(tensor * ROWS, ROWS), ROWS), :]
    for copy in peer_copies:
        copy.wait_recv()

    @pl.loop(0, D_WIN // 512, unroll=2)
    def _(i):
        columns = pl.ds(pl.multiple_of(i * 512, 512), 512)
        acc = from_peers[0, :, columns].astype(F32)
        for t in range(1, PEERS):
            acc += from_peers[t, :, columns].astype(F32)
        summed[:, columns] = acc.astype(BF16)

    store_summed = pltpu.make_async_copy(summed, summed_out, store_sems.at[0])
    store_summed.start()

    for copy in s_mid_copies:
        copy.wait_recv()
    s_chunk = s_mid[0]
    for g in range(1, CHIPS // S_WIN):
        s_chunk += s_mid[g]
    s_full[s_mine] = s_chunk
    s_gathers = []
    for k, (e, on) in enumerate(s_targets):
        copy = remote(
            s_full.at[s_mine], s_full.at[s_mine], s_gather_s.at[k], s_gather_r.at[k], at(-sign * e, on)
        )
        copy.start()
        s_gathers.append(copy)
    for k in reversed(range(len(s_targets))):
        e, on = s_targets[k]
        toward = sign * e if k < len(S_NEAR) else -sign * e
        i = s_chunk_of(chip_at(toward), on)
        remote(
            s_full.at[i], s_full.at[i], s_gather_s.at[k], s_gather_r.at[k], at(toward, on)
        ).wait_recv()

    both = dot(apply_ref[...], s_full[...].reshape(RANK, COLS), ((1,), (0,)), highest)
    right_high, right_low = halves(both[RANK:])
    right_parts[...] = jnp.concatenate([right_high, right_low], axis=0)
    store_right = pltpu.make_async_copy(right_parts, right_out, store_sems.at[4])
    store_right.start()
    q_out[...] = both[:RANK]
    store_q = pltpu.make_async_copy(q_out, q_sum_out, store_sems.at[1])
    store_q.start()

    for copy in swaps + pairs + sends + mid_copies + gathers + passes + peer_copies + s_sends + s_mid_copies + s_gathers:
        copy.wait_send()
    for copy in (store_summed, store_gradient, store_p_cols, store_right, store_q):
        copy.wait()


def finish(
    summed, q_summed, right_parts, gradient, p_cols, summed_hbm, q_hbm, error_hbm, error, sems
):
    store_summed = pltpu.make_async_copy(summed, summed_hbm, sems.at[0])
    store_q = pltpu.make_async_copy(q_summed, q_hbm, sems.at[1])
    store_summed.start()
    store_q.start()
    stores = []
    for g in range(WIN):
        for b in range(2 * g, 2 * g + 2):
            product = dot(p_cols[b], right_parts[...], ((1,), (0,)))
            error[pl.ds(b * BLK, BLK), :] = (gradient[b] - product).astype(BF16)
        rows = pl.ds(g * 2 * BLK, 2 * BLK)
        stores.append(pltpu.make_async_copy(error.at[rows], error_hbm.at[rows], sems.at[2 + g]))
        stores[-1].start()
    for copy in [store_summed, store_q] + stores:
        copy.wait()


def shards(activations, out_grads, query_weight, carried_q):
    in_hbm = pl.BlockSpec(memory_space=pltpu.HBM)
    dma = pltpu.SemaphoreType.DMA
    near, far, s_near, s_far = len(NEAR), len(FAR), 2 * len(S_NEAR) + 1, len(S_FAR)
    passed = (
        jax.ShapeDtypeStruct((ROWS, D_WIN), BF16),
        jax.ShapeDtypeStruct((RANK, COLS), F32),
        jax.ShapeDtypeStruct((2 * RANK, COLS), BF16),
        jax.ShapeDtypeStruct((2 * WIN, BLK, COLS), F32),
        jax.ShapeDtypeStruct((2 * WIN, BLK, 2 * RANK), BF16),
    )
    operands = (activations, out_grads, query_weight, carried_q.T)
    inputs = [pltpu.with_memory_space_constraint(x, pltpu.HBM) for x in operands]
    results = pl.pallas_call(
        kernel,
        out_shape=passed,
        in_specs=[in_hbm] * 4,
        out_specs=(pl.BlockSpec(memory_space=pl.ANY),) * len(passed),
        scratch_shapes=[
            pltpu.VMEM((2, WIN, TOK, BLK), BF16),
            pltpu.VMEM((WIN, TOK, BLK), BF16),
            pltpu.VMEM((TOK, COLS), BF16),
            pltpu.VMEM((TOK, COLS), BF16),
            pltpu.VMEM((D_WIN, COLS), BF16),
            pltpu.VMEM((RANK, COLS), F32),
            pltpu.VMEM((2 * WIN, BLK, COLS), F32),
            pltpu.VMEM((TOK, D_WIN), BF16),
            pltpu.VMEM((PEERS, ROWS, D_WIN), BF16),
            pltpu.VMEM((ROWS, D_WIN), BF16),
            pltpu.VMEM((PIECES, WIN, HALF, BLK), BF16),
            pltpu.VMEM((PIECES, WIN, HALF, BLK), F32),
            pltpu.VMEM((PIECES, WIN, HALF, BLK), BF16),
            pltpu.VMEM((PIECES, near, HALF, BLK), BF16),
            pltpu.VMEM((PIECES, near, HALF, BLK), BF16),
            pltpu.VMEM((PIECES, GROUPS, HALF, BLK), BF16),
            pltpu.VMEM((2, WIN, PIECES, HALF, BLK), BF16),
            pltpu.VMEM((2 * WIN, BLK, 2 * RANK), BF16),
            pltpu.VMEM((RANK, 2 * TOK), F32),
            pltpu.VMEM((RANK, RANK), F32),
            pltpu.VMEM((RANK, 2 * RANK), F32),
            pltpu.VMEM((2 * RANK, RANK), F32),
            pltpu.VMEM((RANK, COLS), F32),
            pltpu.VMEM((s_near, S_ROWS, COLS), F32),
            pltpu.VMEM((CHIPS // S_WIN, S_ROWS, COLS), F32),
            pltpu.VMEM((2 * S_WIN, S_ROWS, COLS), F32),
            pltpu.VMEM((2 * RANK, COLS), BF16),
            pltpu.VMEM((RANK, COLS), F32),
            dma((3,)), dma((2 * WIN,)), dma((5,)),
            dma((PEERS - 1,)), dma((PEERS - 1,)),
            dma((2,)), dma((2,)),
            dma((PIECES,)), dma((PIECES,)),
            dma((PIECES, near)), dma((PIECES, near)),
            dma((PIECES, far)), dma((PIECES, far)),
            dma((PIECES, near)), dma((PIECES, near)),
            dma((PIECES, near + 1)), dma((PIECES, near + 1)),
            dma((s_near,)), dma((s_near,)),
            dma((s_far,)), dma((s_far,)),
            dma((s_near,)), dma((s_near,)),
            pltpu.SemaphoreType.REGULAR,
        ],
        compiler_params=pltpu.CompilerParams(
            collective_id=0, has_side_effects=True, vmem_limit_bytes=28 * 1024 * 1024
        ),
        name="powersgd",
    )(*inputs)
    summed, q_summed, error = pl.pallas_call(
        finish,
        out_shape=(passed[0], passed[1], jax.ShapeDtypeStruct((D_WIN, COLS), BF16)),
        in_specs=[pl.BlockSpec(memory_space=pltpu.VMEM)] * len(passed),
        out_specs=(pl.BlockSpec(memory_space=pl.ANY),) * 3,
        scratch_shapes=[pltpu.VMEM((D_WIN, COLS), BF16), dma((2 + WIN,))],
        compiler_params=pltpu.CompilerParams(vmem_limit_bytes=24 * 1024 * 1024),
        name="finish",
    )(*results)
    return summed, q_summed.T, error[None]


def solution(mesh):
    in_specs = (P("replica", None), P("replica", "tensor"), P(None, "tensor"), P("tensor", None))
    out_specs = (P(("replica", "tensor"), None), P("tensor", None), P("replica", None, "tensor"))
    return jax.shard_map(shards, mesh=mesh, in_specs=in_specs, out_specs=out_specs, check_vma=False)
```
